32 devices in a mesh: groups: 2 (over x), ctx: 4 (over y, core), head: 4 (over z).
Axes of the slice: x: 2, y: 2, z: 4, core: 2. Of those that a mesh axis runs over, the one named last changes fastest.
Arguments:
- hidden: bfloat16 [2, 2048, 4096], P(None, ('groups', 'ctx'), 'head'), parts along dimension 1, may hold values from -40 to 40
- strand_bases: int32 [2048], P(('groups', 'ctx')), parts along dimension 0, may hold values from 0 to 3
- variant_sites: int32 [256], P('groups'), parts along dimension 0, may hold values from 0 to 1023, as said below
- base_shift: int32 [256], P('groups'), parts along dimension 0, may hold values from 1 to 3
- base_embed: bfloat16 [4, 4096], replicated, may hold values from -6 to 6
- query_weight: bfloat16 [4096, 2048], P(None, 'head')
- key_weight: bfloat16 [4096, 2048], P(None, 'head')
- value_weight: bfloat16 [4096, 2048], P(None, 'head'), may hold values from -0.09375 to 0.09375
- out_weight: bfloat16 [2048, 4096], P('head'), may hold values from -4 to 4
Outputs:
- mixed: bfloat16 [2048, 4096], P(('groups', 'ctx'), 'head'), parts along dimension 0
The draws below stay inside these ranges and needn't reach their ends.
There are 2 independent parts, one for each index of `groups`. The reference program is written for one: setup_inputs(seed, part) draws one part's arguments, and reference() takes and returns one part's arrays. A program takes and returns all parts, laid end to end along the dimension named above; an argument that names none is the same for every part. Nothing has to cross between parts.
Inputs may be any that keep to these rules, and one draw needn't show every extreme that they name: `variant_sites`: distinct positions; each aligned block of 256 positions holds at most 64 of them, and some block holds exactly that many.
All inputs are finite; a program needn't handle non-finite values.
Results may differ from the reference program's by a relative error of at most 0.019.
Values may be sent and summed in bfloat16 or wider, within the bound.
No kernel may reach another device: no remote copies, remote signals or barrier semaphores. Data moves between devices by JAX's collectives and lax.ppermute only.
A program may use at most 128 MiB of HBM per device.

```python
import math
import jax
import jax.numpy as jnp
from jax import lax

D = 4096
HEAD_DIM = 128
HEADS = 16
ROWS_DEV = 256
VAR_DEV = 32
SEQ_LEN = 1024
VARS = 128


def draw_hidden(key, part):
    base_draw = jax.random.truncated_normal(jax.random.fold_in(key, 41), -6.0, 6.0, (2, SEQ_LEN, D), jnp.float32)
    base_draw = jnp.clip(base_draw, -40.0, 40.0)
    return base_draw.astype(jnp.bfloat16)


def shared_weights(key):
    head_width = HEADS * HEAD_DIM
    shared = jax.random.truncated_normal(jax.random.fold_in(key, 31), -4.0, 4.0, (D, head_width), jnp.float32) / math.sqrt(D)
    private = jax.random.truncated_normal(jax.random.fold_in(key, 32), -4.0, 4.0, (D, head_width), jnp.float32) / math.sqrt(D)
    return (shared, private)


def draw_query_weight(key, part):
    shared, private = shared_weights(key)
    return shared.astype(jnp.bfloat16)


def draw_key_weight(key, part):
    shared, private = shared_weights(key)
    result = private
    return result.astype(jnp.bfloat16)


def draw_variant_sites(key, part):
    block_total = SEQ_LEN // ROWS_DEV
    slot_cap = 2 * VAR_DEV
    key_order = jax.random.fold_in(key, 51)
    key_shift = jax.random.fold_in(key, 52)
    key_rows = jax.random.fold_in(key, 53)
    key_mix = jax.random.fold_in(key, 54)
    block_order = jax.random.permutation(key_order, block_total)
    shifts = jax.random.randint(key_shift, (block_total // 2,), 0, VAR_DEV + 1)
    shifts = shifts.at[0].set(VAR_DEV)
    signed = jnp.concatenate([shifts, -shifts])
    counts = jnp.zeros((block_total,), jnp.int32).at[block_order].set(VAR_DEV + signed)
    row_keys = jax.random.split(key_rows, block_total)
    row_perm = jax.vmap(lambda sub_key: jax.random.permutation(sub_key, ROWS_DEV))(row_keys)[:, :slot_cap]
    positions = (jnp.arange(block_total, dtype=jnp.int32)[:, None] * ROWS_DEV + row_perm).reshape(-1)
    is_valid = (jnp.arange(slot_cap, dtype=jnp.int32)[None, :] < counts[:, None]).reshape(-1)
    ranked = jnp.argsort(jnp.where(is_valid, 0, 1), stable=True)[:VARS]
    chosen = positions[ranked]
    shuffle = jax.random.permutation(key_mix, VARS)
    return chosen[shuffle].astype(jnp.int32)


def touch_ends(values, own_key, low, high):
    index_at = [jax.random.randint(jax.random.fold_in(own_key, axis), (), 0, length) for axis, length in enumerate(values.shape)]
    main_axis = values.shape.index(max(values.shape))
    beside = index_at[:main_axis] + [(index_at[main_axis] + 1) % values.shape[main_axis]] + index_at[main_axis + 1:]
    return values.at[tuple(index_at)].set(low).at[tuple(beside)].set(high)


def shard_levels(own_key, shape, shards, least, top_value):
    def one(axis_at, shards_of):
        draws = jax.random.uniform(jax.random.fold_in(jax.random.fold_in(own_key, 6), axis_at), (shards_of,), jnp.float32, least / len(shards), top_value / len(shards))
        return jnp.repeat(jnp.exp(draws), shape[axis_at] // shards_of).reshape((-1,) + (1,) * (len(shape) - axis_at - 1))

    factor_of = one(*shards[0])
    for cut in shards[1:]:
        factor_of = factor_of * one(*cut)
    return factor_of


def bell_draw(stream_key, shape, deviation, limit, cuts=(), kind=jnp.bfloat16):
    array = deviation * jax.random.normal(stream_key, shape, jnp.float32)
    if cuts:
        array = array * shard_levels(stream_key, shape, cuts, -0.22, 0.18)
    return jnp.clip(array, -limit, limit).astype(kind)


def setup_inputs(seed: int = 0, part: int = 0) -> dict:
    arg_keys = jax.random.split(jax.random.key(seed), 10)
    own_keys = jax.random.split(jax.random.fold_in(arg_keys[9], part), 10)
    hidden = draw_hidden(jax.random.fold_in(jax.random.fold_in(arg_keys[9], part), 71), part)
    strand_bases = touch_ends(jax.random.randint(own_keys[1], (SEQ_LEN,), 0, 4), jax.random.fold_in(own_keys[1], 1), 0, 3).astype(jnp.int32)
    variant_sites = draw_variant_sites(jax.random.fold_in(jax.random.fold_in(arg_keys[9], part), 71), part)
    base_shift = touch_ends(jax.random.randint(own_keys[3], (VARS,), 1, 4), jax.random.fold_in(own_keys[3], 1), 1, 3).astype(jnp.int32)
    base_embed = bell_draw(arg_keys[4], (4, D), 1.0, 6.0)
    query_weight = draw_query_weight(jax.random.fold_in(arg_keys[9], 71), part)
    key_weight = draw_key_weight(jax.random.fold_in(arg_keys[9], 71), part)
    value_weight = bell_draw(arg_keys[7], (D, HEADS * HEAD_DIM), D ** -0.5, 0.09375, ((1, 4),))
    out_weight = bell_draw(arg_keys[8], (HEADS * HEAD_DIM, D), 2 ** -0.5, 4.0, ((0, 4),))
    return dict(hidden=hidden, strand_bases=strand_bases, variant_sites=variant_sites, base_shift=base_shift, base_embed=base_embed, query_weight=query_weight, key_weight=key_weight, value_weight=value_weight, out_weight=out_weight)


ROPE_BASE = 10000.0

def rotate(values, positions):
    half_dim = values.shape[-1] // 2
    freq_table = jnp.power(ROPE_BASE, -jnp.arange(half_dim, dtype=jnp.float32) * 2.0 / values.shape[-1])
    angle_grid = positions[:, None] * freq_table[None, :]
    cos_part = jnp.cos(angle_grid)[:, None, :]
    sin_part = jnp.sin(angle_grid)[:, None, :]
    lower_half = values[..., :half_dim]
    upper_half = values[..., half_dim:]
    return jnp.concatenate([lower_half * cos_part - upper_half * sin_part, upper_half * cos_part + lower_half * sin_part], axis=-1)

def project_rows(inputs, weight, positions, rotated):
    n_rows = inputs.shape[0]
    product = jnp.dot(inputs, weight, preferred_element_type=jnp.float32)
    product = product.reshape(n_rows, -1, HEAD_DIM)
    if rotated:
        product = rotate(product, positions)
    return product.astype(jnp.bfloat16)

def attend(queries, keys_in, values_in, forward):
    window_iota = jnp.arange(SEQ_LEN, dtype=jnp.int32)
    if forward:
        allowed = window_iota[None, :] <= window_iota[:, None]
    else:
        allowed = window_iota[None, :] >= window_iota[:, None]

    def one_head(operands):
        head_query, head_key, head_value = operands
        scores = jnp.dot(head_query, head_key.T, preferred_element_type=jnp.float32) / math.sqrt(HEAD_DIM)
        masked = jnp.where(allowed, scores, -jnp.inf)
        row_max = lax.optimization_barrier(jnp.max(masked, axis=1, keepdims=True))
        weights = jnp.where(allowed, jnp.exp(scores - row_max), 0.0)
        weights = weights / lax.optimization_barrier(jnp.sum(weights, axis=1, keepdims=True))
        return jnp.dot(weights.astype(jnp.bfloat16), head_value, preferred_element_type=jnp.float32)
    return lax.map(one_head, (queries.transpose(1, 0, 2), keys_in.transpose(1, 0, 2), values_in.transpose(1, 0, 2)))

def reference(hidden, strand_bases, variant_sites, base_shift, base_embed, query_weight, key_weight, value_weight, out_weight):
    embed_table = base_embed.astype(jnp.float32)
    old_base = strand_bases[variant_sites]
    new_base = (old_base + base_shift) % 4
    plus_diff = embed_table[new_base] - embed_table[old_base]
    minus_diff = embed_table[3 - new_base] - embed_table[3 - old_base]
    window_pos = jnp.arange(SEQ_LEN, dtype=jnp.float32)
    plus_pos = window_pos
    minus_pos = SEQ_LEN - 1 - window_pos
    plus_rows = (hidden[0][variant_sites].astype(jnp.float32) + plus_diff).astype(jnp.bfloat16)
    minus_rows = (hidden[1][variant_sites].astype(jnp.float32) + minus_diff).astype(jnp.bfloat16)
    mutant_plus = hidden[0].at[variant_sites].set(plus_rows)
    mutant_minus = hidden[1].at[variant_sites].set(minus_rows)
    outcomes = []
    for inputs, positions, forward in ((hidden[0], plus_pos, True), (mutant_plus, plus_pos, True), (hidden[1], minus_pos, False), (mutant_minus, minus_pos, False)):
        queries = project_rows(inputs, query_weight, positions, True)
        keys_out = project_rows(inputs, key_weight, positions, True)
        values_out = project_rows(inputs, value_weight, positions, False)
        outcomes.append(attend(queries, keys_out, values_out, forward))
    combined = 0.5 * (outcomes[0] - outcomes[1] + (outcomes[2] - outcomes[3]))
    combined = combined.transpose(1, 0, 2).reshape(SEQ_LEN, -1).astype(jnp.bfloat16)
    return jnp.dot(combined, out_weight, preferred_element_type=jnp.float32).astype(jnp.bfloat16)
```

```python
import functools
import math

import jax
import jax.numpy as jnp
from jax import lax
from jax.experimental import pallas as pl
from jax.experimental.pallas import tpu as pltpu
from jax.sharding import PartitionSpec as P

HEAD_DIM = 128
BASES = 4
BASE_PAD = 16
ROPE_BASE = 10000.0
NEG_FILL = -1e30
VMEM_LIMIT = 40 * 1024 * 1024
F32 = jnp.float32
BF16 = jnp.bfloat16


def params():
    return pltpu.CompilerParams(vmem_limit_bytes=VMEM_LIMIT)


def rope_tables(positions):
    half = HEAD_DIM // 2
    freq = jnp.power(ROPE_BASE, -jnp.arange(half, dtype=F32) * 2.0 / HEAD_DIM)
    angle = positions[:, None] * freq[None, :]
    cos, sin = jnp.cos(angle), jnp.sin(angle)
    return jnp.concatenate([cos, cos], axis=1), jnp.concatenate([-sin, sin], axis=1)


def turned(value, cos, sin):
    return value * cos + pltpu.roll(value, HEAD_DIM // 2, axis=1) * sin


def mixed_rows(codes, table):
    total = codes[:, 0:1] * table[0:1, :]
    for base in range(1, BASES):
        total = total + codes[:, base : base + 1] * table[base : base + 1, :]
    return total


def embed_kernel(embed_ref, wq_ref, wk_ref, wv_ref, out_ref):
    width = wq_ref.shape[1]

    @pl.when(pl.program_id(0) == 0)
    def _():
        out_ref[...] = jnp.zeros_like(out_ref)

    for index, weight in enumerate((wq_ref, wk_ref, wv_ref)):
        out_ref[:, index * width : (index + 1) * width] += jnp.dot(
            embed_ref[...], weight[...], preferred_element_type=F32
        )


def embed_project(embed, wq, wk, wv):
    depth, width = wq.shape
    tile = min(512, depth)
    weight_spec = pl.BlockSpec((tile, width), lambda i: (i, 0))
    return pl.pallas_call(
        embed_kernel,
        grid=(depth // tile,),
        in_specs=[pl.BlockSpec((BASE_PAD, tile), lambda i: (0, i))] + [weight_spec] * 3,
        out_specs=pl.BlockSpec((BASE_PAD, 3 * width), lambda i: (0, 0)),
        out_shape=jax.ShapeDtypeStruct((BASE_PAD, 3 * width), F32),
        compiler_params=params(),
        cost_estimate=pl.CostEstimate(
            flops=2 * BASE_PAD * depth * 3 * width,
            bytes_accessed=3 * depth * width * 2,
            transcendentals=0,
        ),
        name="embed_project",
    )(embed, wq, wk, wv)


def project_kernel(
    x_ref, wq_ref, wk_ref, wv_ref, ew_ref, codes_ref, cos_ref, sin_ref, q_ref, qm_ref, kv_ref, acc
):
    width = wq_ref.shape[1]
    step = pl.program_id(0)

    @pl.when(step == 0)
    def _():
        acc[...] = jnp.zeros_like(acc)

    rows = x_ref[...]
    for index, weight in enumerate((wq_ref, wk_ref, wv_ref)):
        acc[:, index * width : (index + 1) * width] += jnp.dot(
            rows, weight[...], preferred_element_type=F32
        )

    @pl.when(step == pl.num_programs(0) - 1)
    def _():
        cos, sin, codes = cos_ref[...], sin_ref[...], codes_ref[...]
        for start in range(0, width, HEAD_DIM):
            cols = slice(start, start + HEAD_DIM)
            query = acc[:, cols]
            change = mixed_rows(codes, ew_ref[0:BASES, cols])
            q_ref[:, cols] = turned(query, cos, sin).astype(BF16)
            qm_ref[:, cols] = turned(query + change, cos, sin).astype(BF16)
            kv_ref[:, cols] = turned(
                acc[:, width + start : width + start + HEAD_DIM], cos, sin
            ).astype(BF16)
        kv_ref[:, width:] = acc[:, 2 * width :].astype(BF16)


def project(x, wq, wk, wv, ew, codes, cos, sin, slabs):
    rows, depth = x.shape
    width = wq.shape[1]
    tile = depth // slabs
    weight_spec = pl.BlockSpec((tile, width), lambda i: (i, 0))

    def whole(shape):
        return pl.BlockSpec(shape, lambda i: (0, 0))

    return pl.pallas_call(
        project_kernel,
        grid=(slabs,),
        in_specs=[pl.BlockSpec((rows, tile), lambda i: (0, i))]
        + [weight_spec] * 3
        + [whole(item.shape) for item in (ew, codes, cos, sin)],
        out_specs=[whole((rows, width)), whole((rows, width)), whole((rows, 2 * width))],
        out_shape=[
            jax.ShapeDtypeStruct((rows, width), BF16),
            jax.ShapeDtypeStruct((rows, width), BF16),
            jax.ShapeDtypeStruct((rows, 2 * width), BF16),
        ],
        scratch_shapes=[pltpu.VMEM((rows, 3 * width), F32)],
        compiler_params=params(),
        cost_estimate=pl.CostEstimate(
            flops=2 * rows * depth * 3 * width,
            bytes_accessed=3 * depth * width * 2 + rows * depth * 2,
            transcendentals=0,
        ),
        name="project",
    )(x, wq, wk, wv, ew, codes, cos, sin)


def attend_kernel(forward, block_count, has_before, *refs):
    (ids_ref, q_ref, qm_ref, ew_ref), refs = refs[:4], refs[4:]
    kv_refs, refs = refs[:block_count], refs[block_count:]
    code_refs, refs = refs[:block_count], refs[block_count:]
    cos_ref, sin_ref = refs[:2]
    refs = refs[2:]
    before_ref = None
    if has_before:
        before_ref, refs = refs[0], refs[1:]
    out_ref, top, total, acc = refs
    rows, width = q_ref.shape
    heads = width // HEAD_DIM
    scale = math.log2(math.e) / math.sqrt(HEAD_DIM)
    my_id = ids_ref[0]

    def block(index):
        kv_ref, code_ref = kv_refs[index], code_refs[index]
        first = pl.multiple_of(ids_ref[index] * rows, rows)
        cos = cos_ref[pl.ds(first, rows), :]
        sin = sin_ref[pl.ds(first, rows), :]
        codes = code_ref[...]
        if index == 0:
            key_at = lax.broadcasted_iota(jnp.int32, (rows, rows), 0)
            query_at = lax.broadcasted_iota(jnp.int32, (rows, rows), 1)
            seen = key_at <= query_at if forward else key_at >= query_at
        for head in range(heads):
            cols = slice(head * HEAD_DIM, (head + 1) * HEAD_DIM)
            key_cols = slice(width + cols.start, width + cols.stop)
            value_cols = slice(2 * width + cols.start, 2 * width + cols.stop)
            key, value = kv_ref[:, cols], kv_ref[:, key_cols]
            key_change = turned(mixed_rows(codes, ew_ref[0:BASES, key_cols]), cos, sin)
            value_change = mixed_rows(codes, ew_ref[0:BASES, value_cols])
            mutant_key = (key.astype(F32) + key_change).astype(BF16)
            mutant_value = (value.astype(F32) + value_change).astype(BF16)
            for kind, (query, keys, values) in enumerate(
                ((q_ref[:, cols], key, value), (qm_ref[:, cols], mutant_key, mutant_value))
            ):
                unit = 2 * head + kind
                area = slice(unit * HEAD_DIM, (unit + 1) * HEAD_DIM)
                scores = lax.dot_general(
                    keys, query, (((1,), (1,)), ((), ())), preferred_element_type=F32
                )
                if index == 0:
                    scores = jnp.where(seen, scores, NEG_FILL)
                peak = jnp.max(scores, axis=0, keepdims=True)
                if index:
                    old_peak = top[unit : unit + 1, :]
                    peak = jnp.maximum(old_peak, peak)
                    fade = jnp.exp2((old_peak - peak) * scale)
                weights = jnp.exp2((scores - peak) * scale)
                if index == 0:
                    weights = jnp.where(seen, weights, 0.0)
                weight_sum = jnp.sum(weights, axis=0, keepdims=True)
                product = lax.dot_general(
                    values,
                    weights.astype(BF16),
                    (((0,), (0,)), ((), ())),
                    preferred_element_type=F32,
                )
                if index:
                    weight_sum = total[unit : unit + 1, :] * fade + weight_sum
                    product = acc[area, :] * fade + product
                top[unit : unit + 1, :] = peak
                total[unit : unit + 1, :] = weight_sum
                acc[area, :] = product

    for index in range(block_count):
        if index == 0:
            block(0)
        else:
            other = ids_ref[index]
            pl.when(other < my_id if forward else other > my_id)(functools.partial(block, index))

    for head in range(heads):
        cols = slice(head * HEAD_DIM, (head + 1) * HEAD_DIM)
        parts = []
        for unit in (2 * head, 2 * head + 1):
            area = slice(unit * HEAD_DIM, (unit + 1) * HEAD_DIM)
            parts.append(acc[area, :] / total[unit : unit + 1, :])
        difference = (parts[0] - parts[1]).T
        if has_before:
            out_ref[:, cols] = (0.5 * (before_ref[:, cols] + difference)).astype(BF16)
        else:
            out_ref[:, cols] = difference


def attend(forward, ids, q, qm, ew, kv_blocks, code_blocks, cos, sin, before=None):
    rows, width = q.shape
    units = 2 * (width // HEAD_DIM)
    vmem = pl.BlockSpec(memory_space=pltpu.VMEM)
    operands = [q, qm, ew, *kv_blocks, *code_blocks, cos, sin]
    if before is not None:
        operands.append(before)
    count = len(kv_blocks)
    return pl.pallas_call(
        functools.partial(attend_kernel, forward, count, before is not None),
        in_specs=[pl.BlockSpec(memory_space=pltpu.SMEM)] + [vmem] * len(operands),
        out_specs=vmem,
        out_shape=jax.ShapeDtypeStruct((rows, width), F32 if before is None else BF16),
        scratch_shapes=[
            pltpu.VMEM((max(units, 8), rows), F32),
            pltpu.VMEM((max(units, 8), rows), F32),
            pltpu.VMEM((units * HEAD_DIM, rows), F32),
        ],
        compiler_params=params(),
        cost_estimate=pl.CostEstimate(
            flops=8 * rows * rows * count * width,
            bytes_accessed=count * rows * width * 4,
            transcendentals=2 * rows * rows * count * (width // HEAD_DIM),
        ),
        name="attend_forward" if forward else "attend_reverse",
    )(ids, *operands)


def out_kernel(rows_ref, weight_ref, out_ref):
    out_ref[0] = jnp.dot(
        rows_ref[...], weight_ref[...], preferred_element_type=F32
    ).astype(BF16)


def out_project(combined, wo, slabs):
    rows, width = combined.shape
    tile = wo.shape[1] // slabs
    return pl.pallas_call(
        out_kernel,
        grid=(slabs,),
        in_specs=[
            pl.BlockSpec((rows, width), lambda i: (0, 0)),
            pl.BlockSpec((width, tile), lambda i: (0, i)),
        ],
        out_specs=pl.BlockSpec((1, rows, tile), lambda i: (i, 0, 0)),
        out_shape=jax.ShapeDtypeStruct((slabs, rows, tile), BF16),
        compiler_params=params(),
        cost_estimate=pl.CostEstimate(
            flops=2 * rows * width * wo.shape[1],
            bytes_accessed=width * wo.shape[1] * 2 + rows * wo.shape[1] * 2,
            transcendentals=0,
        ),
        name="out_project",
    )(combined, wo)


def shards(
    hidden,
    strand_bases,
    variant_sites,
    base_shift,
    base_embed,
    query_weight,
    key_weight,
    value_weight,
    out_weight,
):
    rows = hidden.shape[1]
    ctx = lax.axis_size("ctx")
    slabs = lax.axis_size("head")
    me = lax.axis_index("ctx")
    window = rows * ctx
    cores = 2 if ctx % 2 == 0 else 1

    def ctx_gather(block):
        held = [block]
        for shift in range(1, ctx // cores):
            pairs = [(i, (i + cores * shift) % ctx) for i in range(ctx)]
            held.append(lax.ppermute(block, "ctx", pairs))
        if cores == 2:
            pairs = [(i, i ^ 1) for i in range(ctx)]
            held = held + [lax.ppermute(item, "ctx", pairs) for item in held]
        return held

    near = [(me - cores * shift) % ctx for shift in range(ctx // cores)]
    if cores == 2:
        near = near + [item ^ 1 for item in near]
    ids = jnp.stack(near).astype(jnp.int32)

    gathered = [
        lax.all_gather(hidden[strand], "head", axis=1, tiled=True) for strand in range(2)
    ]

    base_blocks = ctx_gather(strand_bases)
    embed = jnp.zeros((BASE_PAD, base_embed.shape[1]), BF16).at[:BASES].set(base_embed)
    ew_plus = embed_project(embed, query_weight, key_weight, value_weight)
    ew_minus = ew_plus.at[:BASES].set(ew_plus[:BASES][::-1])

    row_iota = jnp.arange(rows, dtype=jnp.int32)
    code_iota = jnp.arange(BASES, dtype=jnp.int32)
    code_blocks = []
    for bases, owner in zip(base_blocks, near):
        match = (owner * rows + row_iota)[:, None] == variant_sites[None, :]
        changed = jnp.any(match, axis=1)
        shift = jnp.sum(jnp.where(match, base_shift[None, :], 0), axis=1)
        fresh = jnp.mod(bases + shift, BASES)
        codes = (fresh[:, None] == code_iota[None, :]).astype(F32) - (
            bases[:, None] == code_iota[None, :]
        ).astype(F32)
        code_blocks.append(jnp.where(changed[:, None], codes, 0.0))

    positions = jnp.arange(window, dtype=jnp.int32)
    tables = [
        rope_tables(positions.astype(F32)),
        rope_tables((window - 1 - positions).astype(F32)),
    ]
    before = None
    for strand in range(2):
        cos, sin = tables[strand]
        ew = ew_plus if strand == 0 else ew_minus
        own_cos = lax.dynamic_slice_in_dim(cos, me * rows, rows, 0)
        own_sin = lax.dynamic_slice_in_dim(sin, me * rows, rows, 0)
        q, qm, kv = project(
            gathered[strand],
            query_weight,
            key_weight,
            value_weight,
            ew,
            code_blocks[0],
            own_cos,
            own_sin,
            slabs,
        )
        kv_blocks = ctx_gather(kv)
        before = attend(
            strand == 0, ids, q, qm, ew, kv_blocks, code_blocks, cos, sin, before
        )
    partial = out_project(before, out_weight, slabs)
    return lax.psum_scatter(partial, "head", scatter_dimension=0, tiled=True)[0]


def solution(mesh):
    return jax.shard_map(
        shards,
        mesh=mesh,
        in_specs=(
            P(None, ("groups", "ctx"), "head"),
            P(("groups", "ctx")),
            P("groups"),
            P("groups"),
            P(),
            P(None, "head"),
            P(None, "head"),
            P(None, "head"),
            P("head", None),
        ),
        out_specs=P(("groups", "ctx"), "head"),
        check_vma=False,
    )
```

```python
import functools
import math

import jax
import jax.numpy as jnp
from jax import lax
from jax.experimental import pallas as pl
from jax.experimental.pallas import tpu as pltpu
from jax.sharding import PartitionSpec as P

HEAD_DIM = 128
BASES = 4
BASE_PAD = 16
ROPE_BASE = 10000.0
NEG_FILL = -1e30
VMEM_LIMIT = 56 * 1024 * 1024
F32 = jnp.float32
BF16 = jnp.bfloat16


def params():
    return pltpu.CompilerParams(vmem_limit_bytes=VMEM_LIMIT)


def rope_tables(positions):
    half = HEAD_DIM // 2
    freq = jnp.power(ROPE_BASE, -jnp.arange(half, dtype=F32) * 2.0 / HEAD_DIM)
    angle = positions[:, None] * freq[None, :]
    cos, sin = jnp.cos(angle), jnp.sin(angle)
    return jnp.concatenate([cos, cos], axis=1), jnp.concatenate([-sin, sin], axis=1)


def turned(value, cos, sin):
    return value * cos + pltpu.roll(value, HEAD_DIM // 2, axis=1) * sin


def mixed_rows(codes, table):
    total = codes[:, 0:1] * table[0:1, :]
    for base in range(1, BASES):
        total = total + codes[:, base : base + 1] * table[base : base + 1, :]
    return total


def embed_kernel(embed_ref, wq_ref, wk_ref, wv_ref, out_ref):
    width = wq_ref.shape[1]

    @pl.when(pl.program_id(0) == 0)
    def _():
        out_ref[...] = jnp.zeros_like(out_ref)

    for index, weight in enumerate((wq_ref, wk_ref, wv_ref)):
        out_ref[:, index * width : (index + 1) * width] += jnp.dot(
            embed_ref[...], weight[...], preferred_element_type=F32
        )


def embed_project(embed, wq, wk, wv):
    depth, width = wq.shape
    tile = min(512, depth)
    weight_spec = pl.BlockSpec((tile, width), lambda i: (i, 0))
    return pl.pallas_call(
        embed_kernel,
        grid=(depth // tile,),
        in_specs=[pl.BlockSpec((BASE_PAD, tile), lambda i: (0, i))] + [weight_spec] * 3,
        out_specs=pl.BlockSpec((BASE_PAD, 3 * width), lambda i: (0, 0)),
        out_shape=jax.ShapeDtypeStruct((BASE_PAD, 3 * width), F32),
        compiler_params=params(),
        cost_estimate=pl.CostEstimate(
            flops=2 * BASE_PAD * depth * 3 * width,
            bytes_accessed=3 * depth * width * 2,
            transcendentals=0,
        ),
        name="embed_project",
    )(embed, wq, wk, wv)


def slab_kernel(has_total, last, slab_ref, x_ref, wq_ref, wk_ref, wv_ref, *refs):
    del slab_ref
    if has_total:
        total_refs, refs = refs[:3], refs[3:]
    if last:
        (ewq_ref, ewk_ref, ewv_ref, codes_ref, cos_ref, sin_ref), refs = refs[:6], refs[6:]
        q_ref, qm_ref, kv_ref = refs
    rows = x_ref[...].reshape(x_ref.shape[-2:])
    sums = []
    for index, weight in enumerate((wq_ref, wk_ref, wv_ref)):
        item = jnp.dot(rows, weight[...], preferred_element_type=F32)
        if has_total:
            item = total_refs[index][...] + item
        sums.append(item)
    if not last:
        for index in range(3):
            refs[index][...] = sums[index]
        return
    cos, sin, codes = cos_ref[...], sin_ref[...], codes_ref[...]
    for start in range(0, wq_ref.shape[1], HEAD_DIM):
        cols = slice(start, start + HEAD_DIM)
        query, key = sums[0][:, cols], sums[1][:, cols]
        change = mixed_rows(codes, ewq_ref[0:BASES, cols])
        q_ref[:, cols] = turned(query, cos, sin).astype(BF16)
        qm_ref[:, cols] = turned(query + change, cos, sin).astype(BF16)
        kv_ref[0, :, cols] = turned(key, cos, sin).astype(BF16)
    kv_ref[1] = sums[2].astype(BF16)


def project_slab(slab, x, strand, weights, total=None, finish=None):
    rows, tile = x.shape[-2:]
    width = weights[0].shape[1]
    cols = min(2 * HEAD_DIM, width)
    if x.ndim == 3:
        x_spec = pl.BlockSpec((1, rows, tile), lambda j, slab: (strand, 0, 0))
    else:
        x_spec = pl.BlockSpec((rows, tile), lambda j, slab: (0, 0))
    in_specs = [x_spec] + [pl.BlockSpec((tile, cols), lambda j, slab: (slab[0], j))] * 3
    operands = [x, *weights]
    sum_spec = pl.BlockSpec((rows, cols), lambda j, slab: (0, j))
    aliases = {}
    if total is not None:
        in_specs += [sum_spec] * 3
        operands += total
        if finish is None:
            aliases = {5 + index: index for index in range(3)}
    if finish is None:
        out_specs = [sum_spec] * 3
        out_shape = [jax.ShapeDtypeStruct((rows, width), F32)] * 3
    else:
        ew, codes, cos, sin = finish
        steps = width // cols
        in_specs += [
            pl.BlockSpec((BASE_PAD, cols), lambda j, slab: (0, j)),
            pl.BlockSpec((BASE_PAD, cols), lambda j, slab: (0, j + steps)),
            pl.BlockSpec((BASE_PAD, cols), lambda j, slab: (0, j + 2 * steps)),
        ] + [pl.BlockSpec(item.shape, lambda j, slab: (0, 0)) for item in (codes, cos, sin)]
        operands += [ew, ew, ew, codes, cos, sin]
        out_specs = [sum_spec, sum_spec, pl.BlockSpec((2, rows, cols), lambda j, slab: (0, 0, j))]
        out_shape = [
            jax.ShapeDtypeStruct((rows, width), BF16),
            jax.ShapeDtypeStruct((rows, width), BF16),
            jax.ShapeDtypeStruct((2, rows, width), BF16),
        ]
    return pl.pallas_call(
        functools.partial(slab_kernel, total is not None, finish is not None),
        grid_spec=pltpu.PrefetchScalarGridSpec(
            num_scalar_prefetch=1,
            grid=(width // cols,),
            in_specs=in_specs,
            out_specs=out_specs,
        ),
        out_shape=out_shape,
        input_output_aliases=aliases,
        compiler_params=params(),
        cost_estimate=pl.CostEstimate(
            flops=6 * rows * tile * width,
            bytes_accessed=6 * tile * width + 2 * rows * tile + 12 * rows * width,
            transcendentals=0,
        ),
        name="project_slab" if finish is None else "project_finish",
    )(slab, *operands)


def attend_kernel(forward, block_count, has_before, *refs):
    (ids_ref, q_ref, qm_ref, ew_ref), refs = refs[:4], refs[4:]
    kv_refs, refs = refs[:block_count], refs[block_count:]
    code_refs, refs = refs[:block_count], refs[block_count:]
    cos_ref, sin_ref = refs[:2]
    refs = refs[2:]
    before_ref = None
    if has_before:
        before_ref, refs = refs[0], refs[1:]
    out_ref, top, total, acc = refs
    rows, width = q_ref.shape
    heads = width // HEAD_DIM
    scale = math.log2(math.e) / math.sqrt(HEAD_DIM)
    my_id = ids_ref[0]

    def block(index):
        kv_ref, code_ref = kv_refs[index], code_refs[index]
        first = pl.multiple_of(ids_ref[index] * rows, rows)
        cos = cos_ref[pl.ds(first, rows), :]
        sin = sin_ref[pl.ds(first, rows), :]
        codes = code_ref[...]
        if index == 0:
            key_at = lax.broadcasted_iota(jnp.int32, (rows, rows), 0)
            query_at = lax.broadcasted_iota(jnp.int32, (rows, rows), 1)
            seen = key_at <= query_at if forward else key_at >= query_at
        for head in range(heads):
            cols = slice(head * HEAD_DIM, (head + 1) * HEAD_DIM)
            key_cols = slice(width + cols.start, width + cols.stop)
            value_cols = slice(2 * width + cols.start, 2 * width + cols.stop)
            key, value = kv_ref[0, :, cols], kv_ref[1, :, cols]
            key_change = turned(mixed_rows(codes, ew_ref[0:BASES, key_cols]), cos, sin)
            value_change = mixed_rows(codes, ew_ref[0:BASES, value_cols])
            mutant_key = (key.astype(F32) + key_change).astype(BF16)
            mutant_value = (value.astype(F32) + value_change).astype(BF16)
            for kind, (query, keys, values) in enumerate(
                ((q_ref[:, cols], key, value), (qm_ref[:, cols], mutant_key, mutant_value))
            ):
                unit = 2 * head + kind
                area = slice(unit * HEAD_DIM, (unit + 1) * HEAD_DIM)
                scores = lax.dot_general(
                    keys, query, (((1,), (1,)), ((), ())), preferred_element_type=F32
                )
                if index == 0:
                    scores = jnp.where(seen, scores, NEG_FILL)
                peak = jnp.max(scores, axis=0, keepdims=True)
                if index:
                    old_peak = top[unit : unit + 1, :]
                    peak = jnp.maximum(old_peak, peak)
                    fade = jnp.exp2((old_peak - peak) * scale)
                weights = jnp.exp2((scores - peak) * scale)
                if index == 0:
                    weights = jnp.where(seen, weights, 0.0)
                weight_sum = jnp.sum(weights, axis=0, keepdims=True)
                product = lax.dot_general(
                    values,
                    weights.astype(BF16),
                    (((0,), (0,)), ((), ())),
                    preferred_element_type=F32,
                )
                if index:
                    weight_sum = total[unit : unit + 1, :] * fade + weight_sum
                    product = acc[area, :] * fade + product
                top[unit : unit + 1, :] = peak
                total[unit : unit + 1, :] = weight_sum
                acc[area, :] = product

    for index in range(block_count):
        if index == 0:
            block(0)
        else:
            other = ids_ref[index]
            pl.when(other < my_id if forward else other > my_id)(functools.partial(block, index))

    for head in range(heads):
        cols = slice(head * HEAD_DIM, (head + 1) * HEAD_DIM)
        parts = []
        for unit in (2 * head, 2 * head + 1):
            area = slice(unit * HEAD_DIM, (unit + 1) * HEAD_DIM)
            parts.append(acc[area, :] / total[unit : unit + 1, :])
        difference = (parts[0] - parts[1]).T
        if has_before:
            out_ref[:, cols] = (0.5 * (before_ref[:, cols] + difference)).astype(BF16)
        else:
            out_ref[:, cols] = difference


def attend(forward, ids, q, qm, ew, kv_blocks, code_blocks, cos, sin, before=None):
    rows, width = q.shape
    units = 2 * (width // HEAD_DIM)
    vmem = pl.BlockSpec(memory_space=pltpu.VMEM)
    operands = [q, qm, ew, *kv_blocks, *code_blocks, cos, sin]
    if before is not None:
        operands.append(before)
    count = len(kv_blocks)
    return pl.pallas_call(
        functools.partial(attend_kernel, forward, count, before is not None),
        in_specs=[pl.BlockSpec(memory_space=pltpu.SMEM)] + [vmem] * len(operands),
        out_specs=vmem,
        out_shape=jax.ShapeDtypeStruct((rows, width), F32 if before is None else BF16),
        scratch_shapes=[
            pltpu.VMEM((max(units, 8), rows), F32),
            pltpu.VMEM((max(units, 8), rows), F32),
            pltpu.VMEM((units * HEAD_DIM, rows), F32),
        ],
        compiler_params=params(),
        cost_estimate=pl.CostEstimate(
            flops=8 * rows * rows * count * width,
            bytes_accessed=count * rows * width * 4,
            transcendentals=2 * rows * rows * count * (width // HEAD_DIM),
        ),
        name="attend_forward" if forward else "attend_reverse",
    )(ids, *operands)


def out_kernel(rows_ref, weight_ref, out_ref):
    out_ref[0] = jnp.dot(
        rows_ref[...], weight_ref[...], preferred_element_type=F32
    ).astype(BF16)


def out_project(combined, wo, slabs):
    rows, width = combined.shape
    tile = wo.shape[1] // slabs
    return pl.pallas_call(
        out_kernel,
        grid=(slabs,),
        in_specs=[
            pl.BlockSpec((rows, width), lambda i: (0, 0)),
            pl.BlockSpec((width, tile), lambda i: (0, i)),
        ],
        out_specs=pl.BlockSpec((1, rows, tile), lambda i: (i, 0, 0)),
        out_shape=jax.ShapeDtypeStruct((slabs, rows, tile), BF16),
        compiler_params=params(),
        cost_estimate=pl.CostEstimate(
            flops=2 * rows * width * wo.shape[1],
            bytes_accessed=width * wo.shape[1] * 2 + rows * wo.shape[1] * 2,
            transcendentals=0,
        ),
        name="out_project",
    )(combined, wo)


def shards(
    hidden,
    strand_bases,
    variant_sites,
    base_shift,
    base_embed,
    query_weight,
    key_weight,
    value_weight,
    out_weight,
):
    rows = hidden.shape[1]
    ctx = lax.axis_size("ctx")
    slabs = lax.axis_size("head")
    me = lax.axis_index("ctx")
    window = rows * ctx
    cores = 2 if ctx % 2 == 0 else 1

    def ctx_gather(block):
        held = [block]
        for shift in range(1, ctx // cores):
            pairs = [(i, (i + cores * shift) % ctx) for i in range(ctx)]
            held.append(lax.ppermute(block, "ctx", pairs))
        if cores == 2:
            pairs = [(i, i ^ 1) for i in range(ctx)]
            held = held + [lax.ppermute(item, "ctx", pairs) for item in held]
        return held

    near = [(me - cores * shift) % ctx for shift in range(ctx // cores)]
    if cores == 2:
        near = near + [item ^ 1 for item in near]
    ids = jnp.stack(near).astype(jnp.int32)

    ring = [(i, (i + 1) % slabs) for i in range(slabs)]
    head = lax.axis_index("head")
    weights = (query_weight, key_weight, value_weight)

    base_blocks = ctx_gather(strand_bases)
    embed = jnp.zeros((BASE_PAD, base_embed.shape[1]), BF16).at[:BASES].set(base_embed)
    ew_plus = embed_project(embed, query_weight, key_weight, value_weight)
    ew_minus = ew_plus.at[:BASES].set(ew_plus[:BASES][::-1])

    row_iota = jnp.arange(rows, dtype=jnp.int32)
    code_iota = jnp.arange(BASES, dtype=jnp.int32)
    code_blocks = []
    for bases, owner in zip(base_blocks, near):
        match = (owner * rows + row_iota)[:, None] == variant_sites[None, :]
        changed = jnp.any(match, axis=1)
        shift = jnp.sum(jnp.where(match, base_shift[None, :], 0), axis=1)
        fresh = jnp.mod(bases + shift, BASES)
        codes = (fresh[:, None] == code_iota[None, :]).astype(F32) - (
            bases[:, None] == code_iota[None, :]
        ).astype(F32)
        code_blocks.append(jnp.where(changed[:, None], codes, 0.0))

    positions = jnp.arange(window, dtype=jnp.int32)
    tables = [
        rope_tables(positions.astype(F32)),
        rope_tables((window - 1 - positions).astype(F32)),
    ]
    before = None
    ring_free = None
    for strand in range(2):
        cos, sin = tables[strand]
        ew = ew_plus if strand == 0 else ew_minus
        own_cos = lax.dynamic_slice_in_dim(cos, me * rows, rows, 0)
        own_sin = lax.dynamic_slice_in_dim(sin, me * rows, rows, 0)
        finish = (ew, code_blocks[0], own_cos, own_sin)
        moving = hidden[strand]
        if ring_free is not None:
            moving, ring_free = lax.optimization_barrier((moving, ring_free))
        total, here = None, hidden
        for step in range(slabs):
            slab = ((head - step) % slabs).astype(jnp.int32)[None]
            if step < slabs - 1:
                moving = lax.ppermute(moving, "head", ring)
            total = project_slab(
                slab, here, strand, weights, total, finish if step == slabs - 1 else None
            )
            here = moving
        ring_free = moving
        q, qm, kv = total
        kv_blocks = ctx_gather(kv)
        before = attend(
            strand == 0, ids, q, qm, ew, kv_blocks, code_blocks, cos, sin, before
        )
    partial = out_project(before, out_weight, slabs)
    return lax.psum_scatter(partial, "head", scatter_dimension=0, tiled=True)[0]


def solution(mesh):
    return jax.shard_map(
        shards,
        mesh=mesh,
        in_specs=(
            P(None, ("groups", "ctx"), "head"),
            P(("groups", "ctx")),
            P("groups"),
            P("groups"),
            P(),
            P(None, "head"),
            P(None, "head"),
            P(None, "head"),
            P("head", None),
        ),
        out_specs=P(("groups", "ctx"), "head"),
        check_vma=False,
    )
```

```python
import functools
import math

import jax
import jax.numpy as jnp
from jax import lax
from jax.experimental import pallas as pl
from jax.experimental.pallas import tpu as pltpu
from jax.sharding import PartitionSpec as P

HEAD_DIM = 128
BASES = 4
CODES = 16
SUM_CODE = 8
ROPE_BASE = 10000.0
NEG_FILL = -1e30
COST_CUT = 64
SCORE_SCALE = math.log2(math.e) / math.sqrt(HEAD_DIM)
VMEM_LIMIT = 56 * 1024 * 1024
F32 = jnp.float32
BF16 = jnp.bfloat16


def params():
    return pltpu.CompilerParams(vmem_limit_bytes=VMEM_LIMIT)


def cost(flops, moved, exps=0):
    return pl.CostEstimate(
        flops=flops // COST_CUT, bytes_accessed=moved // COST_CUT, transcendentals=exps // COST_CUT
    )


def dot(left, right):
    return jnp.dot(left, right, preferred_element_type=F32)


def rope_tables(positions):
    half = HEAD_DIM // 2
    freq = jnp.power(ROPE_BASE, -jnp.arange(half, dtype=F32) * 2.0 / HEAD_DIM)
    angle = positions[:, None] * freq[None, :]
    cos, sin = jnp.cos(angle), jnp.sin(angle)
    return jnp.concatenate([cos, cos], axis=1), jnp.concatenate([-sin, sin], axis=1)


def swapped(value):
    return pltpu.roll(value, HEAD_DIM // 2, axis=1)


def turned(value, cos, sin):
    return value * cos + swapped(value) * sin


def code_table(rows):
    high = rows.astype(BF16)
    low = (rows - high.astype(F32)).astype(BF16)
    at = lax.broadcasted_iota(jnp.int32, rows.shape, 0)
    return jnp.where(at < BASES, high.astype(F32), low.astype(F32)).astype(BF16)


def read_rows(refs):
    parts = [ref[...].reshape(ref.shape[-2:]) for ref in refs]
    return parts[0] if len(parts) == 1 else jnp.concatenate(parts, axis=0)


def x_spec(x, strand):
    if x.ndim == 3:
        return pl.BlockSpec((1, *x.shape[1:]), lambda j, s: (strand, 0, 0))
    return pl.BlockSpec(x.shape, lambda j, s: (0, 0))


def slab_kernel(slab_parts, with_embed, has_total, scalars, *refs):
    del scalars
    sums = [None] * (6 if with_embed else 3)

    def add(index, item):
        sums[index] = item if sums[index] is None else sums[index] + item

    for parts in slab_parts:
        x_refs, refs = refs[:parts], refs[parts:]
        weights, refs = refs[:3], refs[3:]
        rows = read_rows(x_refs)
        if with_embed:
            embed, refs = refs[0][...], refs[1:]
        for index, weight in enumerate(weights):
            add(index, dot(rows, weight[...]))
            if with_embed:
                add(3 + index, dot(embed, weight[...]))
    if has_total:
        for index in range(len(sums)):
            sums[index] = refs[index][...] + sums[index]
        refs = refs[len(sums) :]
    for ref, item in zip(refs, sums):
        ref[...] = item


def slab_sums(slabs, scalars, strand, weights, embed=None, total=None):
    width = weights[0].shape[1]
    cols = min(2 * HEAD_DIM, width)
    tile = slabs[0][0].shape[-1]
    rows = sum(x.shape[-2] for x in slabs[0])
    in_specs, operands = [], []
    for index, parts in enumerate(slabs):
        in_specs += [x_spec(x, strand) for x in parts]
        in_specs += [pl.BlockSpec((tile, cols), lambda j, s, index=index: (s[index], j))] * 3
        operands += [*parts, *weights]
        if embed is not None:
            in_specs.append(pl.BlockSpec((CODES, tile), lambda j, s, index=index: (0, s[index])))
            operands.append(embed)
    heights = [rows] * 3 + ([CODES] * 3 if embed is not None else [])
    sum_specs = [pl.BlockSpec((height, cols), lambda j, s: (0, j)) for height in heights]
    aliases = {}
    if total is not None:
        aliases = {1 + len(operands) + index: index for index in range(len(heights))}
        in_specs += sum_specs
        operands += total
    return pl.pallas_call(
        functools.partial(
            slab_kernel, [len(parts) for parts in slabs], embed is not None, total is not None
        ),
        grid_spec=pltpu.PrefetchScalarGridSpec(
            num_scalar_prefetch=1,
            grid=(width // cols,),
            in_specs=in_specs,
            out_specs=sum_specs,
        ),
        out_shape=[jax.ShapeDtypeStruct((height, width), F32) for height in heights],
        input_output_aliases=aliases,
        compiler_params=params(),
        cost_estimate=cost(
            6 * rows * tile * width * len(slabs), 6 * tile * width * len(slabs) + 20 * rows * width
        ),
        name="slab_sums",
    )(scalars, *operands)


def finish_kv_kernel(parts, with_embed, scalars, *refs):
    del scalars
    x_refs, refs = refs[:parts], refs[parts:]
    (wk_ref, wv_ref, ksum_ref, vsum_ref, cos_ref, sin_ref), refs = refs[:6], refs[6:]
    if with_embed:
        (embed_ref, ek_ref, ev_ref), refs = refs[:3], refs[3:]
    kv_ref = refs[0]
    rows = read_rows(x_refs)
    cos, sin = cos_ref[...], sin_ref[...]
    key = ksum_ref[...] + dot(rows, wk_ref[...])
    for start in range(0, key.shape[1], HEAD_DIM):
        cols = slice(start, start + HEAD_DIM)
        kv_ref[0, :, cols] = turned(key[:, cols], cos, sin).astype(BF16)
    kv_ref[1] = (vsum_ref[...] + dot(rows, wv_ref[...])).astype(BF16)
    if with_embed:
        _, table_ref, swapped_ref, ev_out = refs
        embed = embed_ref[...]
        ek = ek_ref[...] + dot(embed, wk_ref[...])
        table_ref[...] = code_table(ek)
        for start in range(0, key.shape[1], HEAD_DIM):
            cols = slice(start, start + HEAD_DIM)
            swapped_ref[:, cols] = code_table(swapped(ek[:, cols]))
        ev_out[...] = ev_ref[...] + dot(embed, wv_ref[...])


def finish_kv(part, cols, x_parts, scalars, wk, wv, ksum, vsum, cos, sin, embed_parts):
    tile = x_parts[0].shape[-1]
    rows = ksum.shape[0]

    def at(height):
        return pl.BlockSpec((height, cols), lambda j, s: (0, part))

    weight_spec = pl.BlockSpec((tile, cols), lambda j, s: (s[0], part))
    table_spec = pl.BlockSpec((rows, HEAD_DIM), lambda j, s: (s[1], 0))
    in_specs = [x_spec(x, 0) for x in x_parts]
    in_specs += [weight_spec, weight_spec, at(rows), at(rows), table_spec, table_spec]
    operands = [*x_parts, wk, wv, ksum, vsum, cos, sin]
    out_specs = [pl.BlockSpec((2, rows, cols), lambda j, s: (0, 0, 0))]
    out_shape = [jax.ShapeDtypeStruct((2, rows, cols), BF16)]
    if embed_parts is not None:
        in_specs += [
            pl.BlockSpec((CODES, tile), lambda j, s: (0, s[0])),
            at(CODES),
            at(CODES),
        ]
        operands += embed_parts
        out_specs += [pl.BlockSpec((CODES, cols), lambda j, s: (0, 0))] * 3
        out_shape += [jax.ShapeDtypeStruct((CODES, cols), kind) for kind in (BF16, BF16, F32)]
    return pl.pallas_call(
        functools.partial(finish_kv_kernel, len(x_parts), embed_parts is not None),
        grid_spec=pltpu.PrefetchScalarGridSpec(
            num_scalar_prefetch=1,
            grid=(1,),
            in_specs=in_specs,
            out_specs=out_specs,
        ),
        out_shape=out_shape,
        compiler_params=params(),
        cost_estimate=cost(4 * rows * tile * cols, 4 * tile * cols + 14 * rows * cols),
        name="finish_kv",
    )(scalars, *operands)


def finish_q_kernel(parts, with_embed, scalars, *refs):
    del scalars
    x_refs, refs = refs[:parts], refs[parts:]
    (wq_ref, qsum_ref, cos_ref, sin_ref, codes_ref, eq_ref), refs = refs[:6], refs[6:]
    eq = eq_ref[...]
    if with_embed:
        embed_ref, q_ref, qm_ref, eq_out = refs
        eq = eq + dot(embed_ref[...], wq_ref[...])
        eq_out[...] = eq
    else:
        q_ref, qm_ref = refs
    cos, sin = cos_ref[...] * SCORE_SCALE, sin_ref[...] * SCORE_SCALE
    query = qsum_ref[...] + dot(read_rows(x_refs), wq_ref[...])
    mutant = query + dot(codes_ref[0], code_table(eq))
    for start in range(0, query.shape[1], HEAD_DIM):
        cols = slice(start, start + HEAD_DIM)
        q_ref[:, cols] = turned(query[:, cols], cos, sin).astype(BF16)
        qm_ref[:, cols] = turned(mutant[:, cols], cos, sin).astype(BF16)


def finish_q(cols, x_parts, scalars, wq, qsum, cos, sin, codes, eq, embed):
    tile = x_parts[0].shape[-1]
    rows, width = qsum.shape

    def at(height):
        return pl.BlockSpec((height, cols), lambda j, s: (0, j))

    table_spec = pl.BlockSpec((rows, HEAD_DIM), lambda j, s: (s[1], 0))
    in_specs = [x_spec(x, 0) for x in x_parts]
    in_specs += [
        pl.BlockSpec((tile, cols), lambda j, s: (s[0], j)),
        at(rows),
        table_spec,
        table_spec,
        pl.BlockSpec((1, rows, CODES), lambda j, s: (0, 0, 0)),
        at(CODES),
    ]
    operands = [*x_parts, wq, qsum, cos, sin, codes, eq]
    out_specs = [at(rows), at(rows)]
    out_shape = [jax.ShapeDtypeStruct((rows, width), BF16)] * 2
    if embed is not None:
        in_specs.append(pl.BlockSpec((CODES, tile), lambda j, s: (0, s[0])))
        operands.append(embed)
        out_specs.append(at(CODES))
        out_shape.append(jax.ShapeDtypeStruct((CODES, width), F32))
    return pl.pallas_call(
        functools.partial(finish_q_kernel, len(x_parts), embed is not None),
        grid_spec=pltpu.PrefetchScalarGridSpec(
            num_scalar_prefetch=1,
            grid=(width // cols,),
            in_specs=in_specs,
            out_specs=out_specs,
        ),
        out_shape=out_shape,
        compiler_params=params(),
        cost_estimate=cost(2 * rows * tile * width, 2 * tile * width + 8 * rows * width),
        name="finish_q",
    )(scalars, *operands)


def attend_kernel(forward, block_count, has_before, *refs):
    (ids_ref, q_ref, qm_ref, table_ref, swapped_ref, ev_ref), refs = refs[:6], refs[6:]
    (codes_ref, codes_t_ref, cos_ref, sin_ref), refs = refs[:4], refs[4:]
    kv_refs, refs = refs[:block_count], refs[block_count:]
    before_ref = None
    if has_before:
        before_ref, refs = refs[0], refs[1:]
    out_ref, top, acc = refs
    rows, cols_here = q_ref.shape
    heads = cols_here // HEAD_DIM
    tall = HEAD_DIM + CODES
    my_id = ids_ref[0]

    def block(index):
        kv_ref = kv_refs[index]
        first = pl.multiple_of(ids_ref[index] * rows, rows)
        cos = cos_ref[pl.ds(first, rows), :]
        sin = sin_ref[pl.ds(first, rows), :]
        codes, codes_t = codes_ref[index], codes_t_ref[index]
        change = dot(codes, table_ref[...])
        change_swapped = dot(codes, swapped_ref[...])
        if index == 0:
            key_at = lax.broadcasted_iota(jnp.int32, (rows, rows), 0)
            query_at = lax.broadcasted_iota(jnp.int32, (rows, rows), 1)
            seen = key_at <= query_at if forward else key_at >= query_at
        for head in range(heads):
            cols = slice(head * HEAD_DIM, (head + 1) * HEAD_DIM)
            key = kv_ref[0, :, cols]
            mutant_key = (
                key.astype(F32) + change[:, cols] * cos + change_swapped[:, cols] * sin
            ).astype(BF16)
            values_t = jnp.concatenate([kv_ref[1, :, cols].T, codes_t], axis=0)
            for kind, (query, keys) in enumerate(
                ((q_ref[:, cols], key), (qm_ref[:, cols], mutant_key))
            ):
                unit = 2 * head + kind
                area = slice(unit * tall, (unit + 1) * tall)
                scores = lax.dot_general(
                    keys, query, (((1,), (1,)), ((), ())), preferred_element_type=F32
                )
                if index == 0:
                    scores = jnp.where(seen, scores, NEG_FILL)
                peak = jnp.max(scores, axis=0, keepdims=True)
                if index:
                    old_peak = top[unit : unit + 1, :]
                    peak = jnp.maximum(old_peak, peak)
                    fade = jnp.exp2(old_peak - peak)
                weights = jnp.exp2(scores - peak).astype(BF16)
                product = dot(values_t, weights)
                if index:
                    product = acc[area, :] * fade + product
                top[unit : unit + 1, :] = peak
                acc[area, :] = product

    for index in range(block_count):
        if index == 0:
            block(0)
        else:
            other = ids_ref[index]
            pl.when(other < my_id if forward else other > my_id)(functools.partial(block, index))

    code_at = lax.broadcasted_iota(jnp.int32, (CODES, HEAD_DIM), 0)
    for head in range(heads):
        cols = slice(head * HEAD_DIM, (head + 1) * HEAD_DIM)
        ev = jnp.where(code_at < BASES, ev_ref[:, cols], 0.0)
        parts = []
        for kind in range(2):
            start = (2 * head + kind) * tall
            value = acc[start : start + HEAD_DIM, :]
            tail = acc[start + HEAD_DIM : start + tall, :]
            if kind:
                value = value + lax.dot_general(
                    ev,
                    tail,
                    (((0,), (0,)), ((), ())),
                    precision=lax.Precision.HIGHEST,
                    preferred_element_type=F32,
                )
            parts.append(value / tail[SUM_CODE : SUM_CODE + 1, :])
        difference = (parts[0] - parts[1]).T
        if has_before:
            out_ref[:, cols] = (0.5 * (before_ref[:, cols] + difference)).astype(BF16)
        else:
            out_ref[:, cols] = difference


def attend(forward, part, cols, ids, q, qm, tables, codes, codes_t, cos, sin, kv_blocks, before):
    rows = q.shape[0]
    heads = cols // HEAD_DIM
    vmem = pl.BlockSpec(memory_space=pltpu.VMEM)
    row_spec = pl.BlockSpec((rows, cols), lambda j: (0, part))

    def whole(item):
        return pl.BlockSpec(item.shape, lambda j: (0,) * item.ndim)

    operands = [*tables, codes, codes_t, cos, sin, *kv_blocks]
    if before is not None:
        operands.append(before)
    count = len(kv_blocks)
    return pl.pallas_call(
        functools.partial(attend_kernel, forward, count, before is not None),
        grid=(1,),
        in_specs=[pl.BlockSpec(memory_space=pltpu.SMEM), row_spec, row_spec]
        + [whole(item) for item in operands],
        out_specs=pl.BlockSpec((rows, cols), lambda j: (0, 0)),
        out_shape=jax.ShapeDtypeStruct((rows, cols), F32 if before is None else BF16),
        scratch_shapes=[
            pltpu.VMEM((max(2 * heads, 8), rows), F32),
            pltpu.VMEM((2 * heads * (HEAD_DIM + CODES), rows), F32),
        ],
        compiler_params=params(),
        cost_estimate=cost(
            8 * rows * rows * count * cols,
            4 * count * rows * cols,
            2 * rows * rows * count * heads,
        ),
        name="attend_forward" if forward else "attend_reverse",
    )(ids, q, qm, *operands)


def out_kernel(has_before, scalars, rows_ref, weight_ref, *refs):
    del scalars
    if has_before:
        before_ref, out_ref, acc = refs
    else:
        out_ref, acc = refs
    step = pl.program_id(0)

    @pl.when(step == 0)
    def _():
        acc[...] = before_ref[...] if has_before else jnp.zeros_like(acc)

    acc[...] += dot(rows_ref[0], weight_ref[0])

    @pl.when(step == pl.num_programs(0) - 1)
    def _():
        out_ref[...] = acc[...].astype(out_ref.dtype)


def out_project(part, gathered, weight, slots, last, before):
    slabs, rows, cols = gathered.shape
    width = weight.shape[2]
    whole = pl.BlockSpec((rows, width), lambda i, s: (0, 0))
    in_specs = [
        pl.BlockSpec((1, rows, cols), lambda i, s: (i, 0, 0)),
        pl.BlockSpec((1, cols, width), lambda i, s: (s[i], part, 0)),
    ]
    operands = [gathered, weight]
    if before is not None:
        in_specs.append(whole)
        operands.append(before)
    return pl.pallas_call(
        functools.partial(out_kernel, before is not None),
        grid_spec=pltpu.PrefetchScalarGridSpec(
            num_scalar_prefetch=1,
            grid=(slabs,),
            in_specs=in_specs,
            out_specs=whole,
            scratch_shapes=[pltpu.VMEM((rows, width), F32)],
        ),
        out_shape=jax.ShapeDtypeStruct((rows, width), BF16 if last else F32),
        compiler_params=params(),
        cost_estimate=cost(2 * slabs * rows * cols * width, 2 * slabs * cols * width),
        name="out_project",
    )(slots, *operands)


def shards(
    hidden,
    strand_bases,
    variant_sites,
    base_shift,
    base_embed,
    query_weight,
    key_weight,
    value_weight,
    out_weight,
):
    rows, tile = hidden.shape[1:]
    ctx = lax.axis_size("ctx")
    slabs = lax.axis_size("head")
    me = lax.axis_index("ctx")
    head = lax.axis_index("head")
    window = rows * ctx
    width = query_weight.shape[1]
    cores = 2 if ctx % 2 == 0 else 1
    chains = 2 if rows % 32 == 0 else 1
    parts = 2 if width % (2 * HEAD_DIM) == 0 else 1
    cols = width // parts
    weights = (query_weight, key_weight, value_weight)
    my_row = me.astype(jnp.int32)
    ring = [(i, (i + 1) % slabs) for i in range(slabs)]
    slab_at = [((head - step) % slabs).astype(jnp.int32) for step in range(slabs)]

    def tie(items, *first):
        return lax.optimization_barrier((items, first))[0]

    def ctx_far(block):
        return [
            lax.ppermute(block, "ctx", [(i, (i + cores * shift) % ctx) for i in range(ctx)])
            for shift in range(1, ctx // cores)
        ]

    def ctx_swap(blocks):
        if cores == 1:
            return []
        return [lax.ppermute(item, "ctx", [(i, i ^ 1) for i in range(ctx)]) for item in blocks]

    def hop(blocks):
        return [lax.ppermute(block, "head", ring) for block in blocks]

    near = [(me - cores * shift) % ctx for shift in range(ctx // cores)]
    if cores == 2:
        near = near + [item ^ 1 for item in near]
    ids = jnp.stack(near).astype(jnp.int32)

    span = rows // chains

    def own_chains(source, strand):
        return [source[strand, chain * span : (chain + 1) * span] for chain in range(chains)]

    moving = hop(own_chains(hidden, 0))

    bases = [strand_bases] + ctx_far(strand_bases)
    bases = jnp.stack(bases + ctx_swap(bases))
    positions = ids[:, None] * rows + jnp.arange(rows, dtype=jnp.int32)[None, :]
    match = positions[:, :, None] == variant_sites[None, None, :]
    shifts = jnp.sum(jnp.where(match, base_shift[None, None, :], 0), axis=2)
    fresh = jnp.mod(bases + shifts, BASES)
    code_iota = jnp.arange(CODES, dtype=jnp.int32)

    def code_arrays(forward):
        want = code_iota % BASES
        want = want if forward else BASES - 1 - want

        def fill(old, new, want, at):
            codes = (new == want).astype(F32) - (old == want).astype(F32)
            codes = jnp.where(at < 2 * BASES, codes, (at == SUM_CODE).astype(F32))
            return codes.astype(BF16)

        return (
            fill(bases[:, :, None], fresh[:, :, None], want, code_iota),
            fill(bases[:, None, :], fresh[:, None, :], want[:, None], code_iota[:, None]),
        )

    embed = jnp.concatenate(
        [base_embed, base_embed, jnp.zeros((CODES - 2 * BASES, base_embed.shape[1]), BF16)]
    )
    window_iota = jnp.arange(window, dtype=jnp.int32)
    rope = [
        rope_tables(window_iota.astype(F32)),
        rope_tables((window - 1 - window_iota).astype(F32)),
    ]

    lanes = lax.axis_size("groups") * ctx
    piece_rows = width // lanes
    lane = lax.axis_index("groups") * ctx + me
    piece = lax.dynamic_slice_in_dim(tie(out_weight, rope, bases, moving), lane * piece_rows, piece_rows, 0)
    pieces = []
    for shift in range(slabs):
        target = (head + shift) % slabs
        item = lax.dynamic_slice_in_dim(piece, target * tile, tile, 1)
        if shift:
            item = lax.ppermute(
                item, "head", [(i, (i + shift) % slabs) for i in range(slabs)]
            )
        pieces.append(item)
    pieces = jnp.stack(pieces)
    out_slabs = lax.all_gather(pieces, ("groups", "ctx"), axis=1, tiled=True)
    out_slots = jnp.stack([(head - i) % slabs for i in range(slabs)]).astype(jnp.int32)

    code_sets = [code_arrays(True), code_arrays(False)]

    def add_slabs(strand, steps, total):
        return slab_sums(
            [[hidden] if step == 0 else arrived[strand][step - 1] for step in steps],
            jnp.stack([slab_at[step] for step in steps]),
            strand,
            weights,
            embed if strand == 0 else None,
            total,
        )

    def run_ring(strand, moving, early):
        total, waiting = None, [0]
        for step in range(1, slabs):
            arrived[strand].append(moving)
            if step < slabs - 1:
                if strand == 0 and early and step > 1:
                    early[0] = (early[0], total)
                first = early.pop(0) if early else None
                moving = hop([tie(block, first) for block in moving])
                waiting.append(step)
                total = add_slabs(strand, waiting, total)
                waiting = []
        if waiting:
            total = add_slabs(strand, waiting, total)
        return total

    def finish(strand, last, total, eq):
        first = strand == 0
        cos, sin = rope[strand]
        scalars = jnp.stack([slab_at[-1], my_row])
        own, far, made = [], [], []
        for part in range(parts):
            out = finish_kv(
                part,
                cols,
                last,
                scalars,
                key_weight,
                value_weight,
                total[1],
                total[2],
                cos,
                sin,
                [embed, total[4], total[5]] if first else None,
            )
            own.append(out[0])
            far.append(ctx_far(out[0]) if first else None)
            made.append(out[1:])
        out = finish_q(
            cols,
            last,
            scalars,
            query_weight,
            total[0],
            cos,
            sin,
            code_sets[strand][0],
            total[3] if first else eq,
            embed if first else None,
        )
        return own, far, made, out

    def spread_out(own, far):
        local = [own] + far
        return local + ctx_swap(local)

    def attend_all(strand, blocks, query, tables, before, ids):
        return [
            attend(
                strand == 0,
                part,
                cols,
                ids,
                query[0],
                query[1],
                tables[part],
                *code_sets[strand],
                *rope[strand],
                blocks[part],
                before[part],
            )
            for part in range(parts)
        ]

    arrived = [[], []]
    total = run_ring(0, moving, [None, (code_sets, pieces)])
    last = arrived[0][-1]
    cut = own_chains(tie(hidden, arrived[0][max(0, slabs - 3)]), 1)
    moving = hop([tie(block, item, total) for block, item in zip(cut, last)])
    own, far, tables, query = finish(0, last, total, None)
    eq = query[2]
    total = run_ring(1, moving, [(own, query)])
    blocks = [spread_out(item, item_far) for item, item_far in zip(own, far)]
    last = tie(arrived[1][-1], blocks)
    own_then, _, _, query_then = finish(1, last, total, eq)
    ids_then = tie(ids, own_then, query_then, out_slabs)
    before = attend_all(0, blocks, query, tables, [None] * parts, ids_then)
    far = [ctx_far(item) for item in own_then]
    blocks = []
    for part in range(parts):
        arriving = tie(far[part], before[: part + 1])
        blocks.append(spread_out(own_then[part], arriving))
    combined = attend_all(1, blocks, query_then, tables, before, ids)
    result = None
    for part in range(parts):
        gathered = lax.all_gather(combined[part], "head", axis=0, tiled=False)
        result = out_project(part, gathered, out_slabs, out_slots, part == parts - 1, result)
    return result


def solution(mesh):
    return jax.shard_map(
        shards,
        mesh=mesh,
        in_specs=(
            P(None, ("groups", "ctx"), "head"),
            P(("groups", "ctx")),
            P("groups"),
            P("groups"),
            P(),
            P(None, "head"),
            P(None, "head"),
            P(None, "head"),
            P("head", None),
        ),
        out_specs=P(("groups", "ctx"), "head"),
        check_vma=False,
    )
```

```python
import functools
import math

import jax
import jax.numpy as jnp
from jax import lax
from jax.experimental import pallas as pl
from jax.experimental.pallas import tpu as pltpu
from jax.sharding import PartitionSpec as P

HEAD_DIM = 128
BASES = 4
CODES = 16
SUM_CODE = 8
ROPE_BASE = 10000.0
NEG_FILL = -1e30
COST_CUT = 64
SCORE_SCALE = math.log2(math.e) / math.sqrt(HEAD_DIM)
VMEM_LIMIT = 24 * 1024 * 1024
F32 = jnp.float32
BF16 = jnp.bfloat16


def params():
    return pltpu.CompilerParams(vmem_limit_bytes=VMEM_LIMIT)


def cost(flops, moved, exps=0):
    return pl.CostEstimate(
        flops=flops // COST_CUT, bytes_accessed=moved // COST_CUT, transcendentals=exps // COST_CUT
    )


def dot(left, right):
    return jnp.dot(left, right, preferred_element_type=F32)


def rope_tables(positions):
    half = HEAD_DIM // 2
    freq = jnp.power(ROPE_BASE, -jnp.arange(half, dtype=F32) * 2.0 / HEAD_DIM)
    angle = positions[:, None] * freq[None, :]
    cos, sin = jnp.cos(angle), jnp.sin(angle)
    return jnp.concatenate([cos, cos], axis=1), jnp.concatenate([-sin, sin], axis=1)


def swapped(value):
    return pltpu.roll(value, HEAD_DIM // 2, axis=1)


def turned(value, cos, sin):
    return value * cos + swapped(value) * sin


def code_table(rows):
    high = rows.astype(BF16)
    low = (rows - high.astype(F32)).astype(BF16)
    at = lax.broadcasted_iota(jnp.int32, rows.shape, 0)
    return jnp.where(at < BASES, high.astype(F32), low.astype(F32)).astype(BF16)


def read_rows(refs):
    parts = [ref[...].reshape(ref.shape[-2:]) for ref in refs]
    return parts[0] if len(parts) == 1 else jnp.concatenate(parts, axis=0)


def x_spec(x, strand):
    if x.ndim == 3:
        return pl.BlockSpec((1, *x.shape[1:]), lambda j, s: (strand, 0, 0))
    return pl.BlockSpec(x.shape, lambda j, s: (0, 0))


def slab_kernel(slab_parts, with_embed, has_total, scalars, *refs):
    del scalars
    sums = [None] * (6 if with_embed else 3)

    def add(index, item):
        sums[index] = item if sums[index] is None else sums[index] + item

    for parts in slab_parts:
        x_refs, refs = refs[:parts], refs[parts:]
        weights, refs = refs[:3], refs[3:]
        rows = read_rows(x_refs)
        if with_embed:
            embed, refs = refs[0][...], refs[1:]
        for index, weight in enumerate(weights):
            add(index, dot(rows, weight[...]))
            if with_embed:
                add(3 + index, dot(embed, weight[...]))
    if has_total:
        for index in range(len(sums)):
            sums[index] = refs[index][...] + sums[index]
        refs = refs[len(sums) :]
    for ref, item in zip(refs, sums):
        ref[...] = item


def slab_sums(slabs, scalars, strand, weights, embed=None, total=None):
    width = weights[0].shape[1]
    cols = min(2 * HEAD_DIM, width)
    tile = slabs[0][0].shape[-1]
    rows = sum(x.shape[-2] for x in slabs[0])
    in_specs, operands = [], []
    for index, parts in enumerate(slabs):
        in_specs += [x_spec(x, strand) for x in parts]
        in_specs += [pl.BlockSpec((tile, cols), lambda j, s, index=index: (s[index], j))] * 3
        operands += [*parts, *weights]
        if embed is not None:
            in_specs.append(pl.BlockSpec((CODES, tile), lambda j, s, index=index: (0, s[index])))
            operands.append(embed)
    heights = [rows] * 3 + ([CODES] * 3 if embed is not None else [])
    sum_specs = [pl.BlockSpec((height, cols), lambda j, s: (0, j)) for height in heights]
    aliases = {}
    if total is not None:
        aliases = {1 + len(operands) + index: index for index in range(len(heights))}
        in_specs += sum_specs
        operands += total
    return pl.pallas_call(
        functools.partial(
            slab_kernel, [len(parts) for parts in slabs], embed is not None, total is not None
        ),
        grid_spec=pltpu.PrefetchScalarGridSpec(
            num_scalar_prefetch=1,
            grid=(width // cols,),
            in_specs=in_specs,
            out_specs=sum_specs,
        ),
        out_shape=[jax.ShapeDtypeStruct((height, width), F32) for height in heights],
        input_output_aliases=aliases,
        compiler_params=params(),
        cost_estimate=cost(
            6 * rows * tile * width * len(slabs), 6 * tile * width * len(slabs) + 20 * rows * width
        ),
        name="slab_sums",
    )(scalars, *operands)


def finish_kv_kernel(parts, with_embed, scalars, *refs):
    del scalars
    x_refs, refs = refs[:parts], refs[parts:]
    (wk_ref, wv_ref, ksum_ref, vsum_ref, cos_ref, sin_ref), refs = refs[:6], refs[6:]
    if with_embed:
        (embed_ref, ek_ref, ev_ref), refs = refs[:3], refs[3:]
    kv_ref = refs[0]
    rows = read_rows(x_refs)
    cos, sin = cos_ref[...], sin_ref[...]
    key = ksum_ref[...] + dot(rows, wk_ref[...])
    for start in range(0, key.shape[1], HEAD_DIM):
        cols = slice(start, start + HEAD_DIM)
        kv_ref[0, :, cols] = turned(key[:, cols], cos, sin).astype(BF16)
    kv_ref[1] = (vsum_ref[...] + dot(rows, wv_ref[...])).astype(BF16)
    if with_embed:
        _, table_ref, swapped_ref, ev_out = refs
        embed = embed_ref[...]
        ek = ek_ref[...] + dot(embed, wk_ref[...])
        table_ref[...] = code_table(ek)
        for start in range(0, key.shape[1], HEAD_DIM):
            cols = slice(start, start + HEAD_DIM)
            swapped_ref[:, cols] = code_table(swapped(ek[:, cols]))
        ev_out[...] = ev_ref[...] + dot(embed, wv_ref[...])


def finish_kv(part, cols, x_parts, scalars, wk, wv, ksum, vsum, cos, sin, embed_parts):
    tile = x_parts[0].shape[-1]
    rows = ksum.shape[0]

    def at(height):
        return pl.BlockSpec((height, cols), lambda j, s: (0, part))

    weight_spec = pl.BlockSpec((tile, cols), lambda j, s: (s[0], part))
    table_spec = pl.BlockSpec((rows, HEAD_DIM), lambda j, s: (s[1], 0))
    in_specs = [x_spec(x, 0) for x in x_parts]
    in_specs += [weight_spec, weight_spec, at(rows), at(rows), table_spec, table_spec]
    operands = [*x_parts, wk, wv, ksum, vsum, cos, sin]
    out_specs = [pl.BlockSpec((2, rows, cols), lambda j, s: (0, 0, 0))]
    out_shape = [jax.ShapeDtypeStruct((2, rows, cols), BF16)]
    if embed_parts is not None:
        in_specs += [
            pl.BlockSpec((CODES, tile), lambda j, s: (0, s[0])),
            at(CODES),
            at(CODES),
        ]
        operands += embed_parts
        out_specs += [pl.BlockSpec((CODES, cols), lambda j, s: (0, 0))] * 3
        out_shape += [jax.ShapeDtypeStruct((CODES, cols), kind) for kind in (BF16, BF16, F32)]
    return pl.pallas_call(
        functools.partial(finish_kv_kernel, len(x_parts), embed_parts is not None),
        grid_spec=pltpu.PrefetchScalarGridSpec(
            num_scalar_prefetch=1,
            grid=(1,),
            in_specs=in_specs,
            out_specs=out_specs,
        ),
        out_shape=out_shape,
        compiler_params=params(),
        cost_estimate=cost(4 * rows * tile * cols, 4 * tile * cols + 14 * rows * cols),
        name="finish_kv",
    )(scalars, *operands)


def finish_q_kernel(parts, with_embed, scalars, *refs):
    del scalars
    x_refs, refs = refs[:parts], refs[parts:]
    (wq_ref, qsum_ref, cos_ref, sin_ref, codes_ref, eq_ref), refs = refs[:6], refs[6:]
    eq = eq_ref[...]
    if with_embed:
        embed_ref, q_ref, qm_ref, eq_out = refs
        eq = eq + dot(embed_ref[...], wq_ref[...])
        eq_out[...] = eq
    else:
        q_ref, qm_ref = refs
    cos, sin = cos_ref[...] * SCORE_SCALE, sin_ref[...] * SCORE_SCALE
    query = qsum_ref[...] + dot(read_rows(x_refs), wq_ref[...])
    mutant = query + dot(codes_ref[0], code_table(eq))
    for start in range(0, query.shape[1], HEAD_DIM):
        cols = slice(start, start + HEAD_DIM)
        q_ref[:, cols] = turned(query[:, cols], cos, sin).astype(BF16)
        qm_ref[:, cols] = turned(mutant[:, cols], cos, sin).astype(BF16)


def finish_q(cols, x_parts, scalars, wq, qsum, cos, sin, codes, eq, embed):
    tile = x_parts[0].shape[-1]
    rows, width = qsum.shape

    def at(height):
        return pl.BlockSpec((height, cols), lambda j, s: (0, j))

    table_spec = pl.BlockSpec((rows, HEAD_DIM), lambda j, s: (s[1], 0))
    in_specs = [x_spec(x, 0) for x in x_parts]
    in_specs += [
        pl.BlockSpec((tile, cols), lambda j, s: (s[0], j)),
        at(rows),
        table_spec,
        table_spec,
        pl.BlockSpec((1, rows, CODES), lambda j, s: (0, 0, 0)),
        at(CODES),
    ]
    operands = [*x_parts, wq, qsum, cos, sin, codes, eq]
    out_specs = [at(rows), at(rows)]
    out_shape = [jax.ShapeDtypeStruct((rows, width), BF16)] * 2
    if embed is not None:
        in_specs.append(pl.BlockSpec((CODES, tile), lambda j, s: (0, s[0])))
        operands.append(embed)
        out_specs.append(at(CODES))
        out_shape.append(jax.ShapeDtypeStruct((CODES, width), F32))
    return pl.pallas_call(
        functools.partial(finish_q_kernel, len(x_parts), embed is not None),
        grid_spec=pltpu.PrefetchScalarGridSpec(
            num_scalar_prefetch=1,
            grid=(width // cols,),
            in_specs=in_specs,
            out_specs=out_specs,
        ),
        out_shape=out_shape,
        compiler_params=params(),
        cost_estimate=cost(2 * rows * tile * width, 2 * tile * width + 8 * rows * width),
        name="finish_q",
    )(scalars, *operands)


def attend_kernel(forward, block_count, has_before, q_start, table_start, before_start, *refs):
    (ids_ref, q_ref, qm_ref, table_ref, swapped_ref, ev_ref), refs = refs[:6], refs[6:]
    (codes_ref, codes_t_ref, cos_ref, sin_ref), refs = refs[:4], refs[4:]
    kv_refs, refs = refs[:block_count], refs[block_count:]
    before_ref = None
    if has_before:
        before_ref, refs = refs[0], refs[1:]
    out_ref, top, acc = refs
    rows, cols_here = out_ref.shape
    heads = cols_here // HEAD_DIM
    tall = HEAD_DIM + CODES
    my_id = ids_ref[0]

    def block(index):
        kv_ref = kv_refs[index]
        first = pl.multiple_of(ids_ref[index] * rows, rows)
        cos = cos_ref[pl.ds(first, rows), :]
        sin = sin_ref[pl.ds(first, rows), :]
        codes, codes_t = codes_ref[index], codes_t_ref[index]
        here = slice(table_start, table_start + cols_here)
        change = dot(codes, table_ref[:, here])
        change_swapped = dot(codes, swapped_ref[:, here])
        if index == 0:
            key_at = lax.broadcasted_iota(jnp.int32, (rows, rows), 0)
            query_at = lax.broadcasted_iota(jnp.int32, (rows, rows), 1)
            seen = key_at <= query_at if forward else key_at >= query_at
        scores, values = [], []
        for head in range(heads):
            cols = slice(head * HEAD_DIM, (head + 1) * HEAD_DIM)
            q_cols = slice(q_start + cols.start, q_start + cols.stop)
            key = kv_ref[0, :, cols]
            mutant_key = (
                key.astype(F32) + change[:, cols] * cos + change_swapped[:, cols] * sin
            ).astype(BF16)
            values.append(jnp.concatenate([kv_ref[1, :, cols].T, codes_t], axis=0))
            for query, keys in ((q_ref[:, q_cols], key), (qm_ref[:, q_cols], mutant_key)):
                scores.append(
                    lax.dot_general(
                        keys, query, (((1,), (1,)), ((), ())), preferred_element_type=F32
                    )
                )
        fades, weights = [], []
        for unit, score in enumerate(scores):
            if index == 0:
                score = jnp.where(seen, score, NEG_FILL)
            peak = jnp.max(score, axis=0, keepdims=True)
            if index:
                old_peak = top[unit : unit + 1, :]
                peak = jnp.maximum(old_peak, peak)
                fades.append(jnp.exp2(old_peak - peak))
            top[unit : unit + 1, :] = peak
            weights.append(jnp.exp2(score - peak).astype(BF16))
        for unit, weight in enumerate(weights):
            area = slice(unit * tall, (unit + 1) * tall)
            product = dot(values[unit // 2], weight)
            acc[area, :] = acc[area, :] * fades[unit] + product if index else product

    for index in range(block_count):
        if index == 0:
            block(0)
        else:
            other = ids_ref[index]
            pl.when(other < my_id if forward else other > my_id)(functools.partial(block, index))

    code_at = lax.broadcasted_iota(jnp.int32, (CODES, HEAD_DIM), 0)
    for head in range(heads):
        cols = slice(head * HEAD_DIM, (head + 1) * HEAD_DIM)
        table_cols = slice(table_start + cols.start, table_start + cols.stop)
        ev = jnp.where(code_at < BASES, ev_ref[:, table_cols], 0.0)
        parts = []
        for kind in range(2):
            start = (2 * head + kind) * tall
            value = acc[start : start + HEAD_DIM, :]
            tail = acc[start + HEAD_DIM : start + tall, :]
            if kind:
                value = value + lax.dot_general(
                    ev,
                    tail,
                    (((0,), (0,)), ((), ())),
                    precision=lax.Precision.HIGHEST,
                    preferred_element_type=F32,
                )
            parts.append(value / tail[SUM_CODE : SUM_CODE + 1, :])
        difference = (parts[0] - parts[1]).T
        if has_before:
            earlier = before_ref[:, before_start + cols.start : before_start + cols.stop]
            out_ref[:, cols] = (0.5 * (earlier + difference)).astype(BF16)
        else:
            out_ref[:, cols] = difference


def attend(forward, start, cols, ids, q, qm, tables, codes, codes_t, cos, sin, kv_blocks, before):
    rows = q.shape[0]
    heads = cols // HEAD_DIM
    vmem = pl.BlockSpec(memory_space=pltpu.VMEM)
    operands = [q, qm, *tables, codes, codes_t, cos, sin, *kv_blocks]
    if before is not None:
        operands.append(before)
    count = len(kv_blocks)
    return pl.pallas_call(
        functools.partial(
            attend_kernel, forward, count, before is not None, start, start, start
        ),
        in_specs=[pl.BlockSpec(memory_space=pltpu.SMEM)] + [vmem] * len(operands),
        out_specs=vmem,
        out_shape=jax.ShapeDtypeStruct((rows, cols), F32 if before is None else BF16),
        scratch_shapes=[
            pltpu.VMEM((max(2 * heads, 8), rows), F32),
            pltpu.VMEM((2 * heads * (HEAD_DIM + CODES), rows), F32),
        ],
        compiler_params=params(),
        cost_estimate=cost(
            8 * rows * rows * count * cols,
            4 * count * rows * cols,
            2 * rows * rows * count * heads,
        ),
        name="attend_forward" if forward else "attend_reverse",
    )(ids, *operands)


def out_kernel(slabs, has_before, *refs):
    row_refs, weight_ref, refs = refs[:slabs], refs[slabs], refs[slabs + 1 :]
    if has_before:
        before_ref, out_ref, acc = refs
    else:
        out_ref, acc = refs
    step = pl.program_id(0)
    for index in range(slabs):

        @pl.when(step == index)
        def _(index=index):
            item = dot(row_refs[index][...], weight_ref[0])
            if index:
                item = acc[...] + item
            elif has_before:
                item = before_ref[...] + item
            if index < slabs - 1:
                acc[...] = item
            else:
                out_ref[...] = item.astype(out_ref.dtype)


def out_project(part, slab_rows, weight, last, before):
    slabs = len(slab_rows)
    rows, cols = slab_rows[0].shape
    width = weight.shape[2]

    def whole(item):
        return pl.BlockSpec(item.shape, lambda i: (0, 0))

    in_specs = [whole(item) for item in slab_rows]
    in_specs.append(pl.BlockSpec((1, cols, width), lambda i: (i, part, 0)))
    operands = [*slab_rows, weight]
    if before is not None:
        in_specs.append(whole(before))
        operands.append(before)
    return pl.pallas_call(
        functools.partial(out_kernel, slabs, before is not None),
        grid=(slabs,),
        in_specs=in_specs,
        out_specs=pl.BlockSpec((rows, width), lambda i: (0, 0)),
        out_shape=jax.ShapeDtypeStruct((rows, width), BF16 if last else F32),
        scratch_shapes=[pltpu.VMEM((rows, width), F32)],
        compiler_params=params(),
        cost_estimate=cost(2 * slabs * rows * cols * width, 2 * slabs * cols * width),
        name="out_project",
    )(*operands)


def shards(
    hidden,
    strand_bases,
    variant_sites,
    base_shift,
    base_embed,
    query_weight,
    key_weight,
    value_weight,
    out_weight,
):
    rows, tile = hidden.shape[1:]
    ctx = lax.axis_size("ctx")
    slabs = lax.axis_size("head")
    me = lax.axis_index("ctx")
    head = lax.axis_index("head")
    window = rows * ctx
    width = query_weight.shape[1]
    cores = 2 if ctx % 2 == 0 else 1
    chains = 2 if rows % 32 == 0 else 1
    parts = 2 if width % (2 * HEAD_DIM) == 0 else 1
    cols = width // parts
    weights = (query_weight, key_weight, value_weight)
    my_row = me.astype(jnp.int32)
    ring = [(i, (i + 1) % slabs) for i in range(slabs)]
    slab_at = [((head - step) % slabs).astype(jnp.int32) for step in range(slabs)]

    def tie(items, *first):
        return lax.optimization_barrier((items, first))[0]

    def ctx_far(block):
        return [
            lax.ppermute(block, "ctx", [(i, (i + cores * shift) % ctx) for i in range(ctx)])
            for shift in range(1, ctx // cores)
        ]

    def ctx_swap(blocks):
        if cores == 1:
            return []
        return [lax.ppermute(item, "ctx", [(i, i ^ 1) for i in range(ctx)]) for item in blocks]

    def hop(blocks):
        return [lax.ppermute(block, "head", ring) for block in blocks]

    near = [(me - cores * shift) % ctx for shift in range(ctx // cores)]
    if cores == 2:
        near = near + [item ^ 1 for item in near]
    ids = jnp.stack(near).astype(jnp.int32)

    span = rows // chains

    def own_chains(source, strand):
        return [source[strand, chain * span : (chain + 1) * span] for chain in range(chains)]

    moving = hop(own_chains(hidden, 0))

    bases = [strand_bases] + ctx_far(strand_bases)
    bases = jnp.stack(bases + ctx_swap(bases))
    positions = ids[:, None] * rows + jnp.arange(rows, dtype=jnp.int32)[None, :]
    match = positions[:, :, None] == variant_sites[None, None, :]
    shifts = jnp.sum(jnp.where(match, base_shift[None, None, :], 0), axis=2)
    fresh = jnp.mod(bases + shifts, BASES)
    code_iota = jnp.arange(CODES, dtype=jnp.int32)

    def code_arrays(forward):
        want = code_iota % BASES
        want = want if forward else BASES - 1 - want

        def fill(old, new, want, at):
            codes = (new == want).astype(F32) - (old == want).astype(F32)
            codes = jnp.where(at < 2 * BASES, codes, (at == SUM_CODE).astype(F32))
            return codes.astype(BF16)

        return (
            fill(bases[:, :, None], fresh[:, :, None], want, code_iota),
            fill(bases[:, None, :], fresh[:, None, :], want[:, None], code_iota[:, None]),
        )

    embed = jnp.concatenate(
        [base_embed, base_embed, jnp.zeros((CODES - 2 * BASES, base_embed.shape[1]), BF16)]
    )
    window_iota = jnp.arange(window, dtype=jnp.int32)
    rope = [
        rope_tables(window_iota.astype(F32)),
        rope_tables((window - 1 - window_iota).astype(F32)),
    ]

    code_sets = [code_arrays(True), code_arrays(False)]

    def add_slabs(strand, steps, total):
        return slab_sums(
            [[hidden] if step == 0 else arrived[strand][step - 1] for step in steps],
            jnp.stack([slab_at[step] for step in steps]),
            strand,
            weights,
            embed if strand == 0 else None,
            total,
        )

    def run_ring(strand, moving, early):
        total, waiting = None, [0]
        partial.clear()
        for step in range(1, slabs):
            arrived[strand].append(moving)
            if step < slabs - 1:
                first = (early.pop(0) if early else None, total)
                moving = hop([tie(block, first) for block in moving])
                waiting.append(step)
                total = add_slabs(strand, waiting, total)
                partial.append(total)
                waiting = []
        if waiting:
            total = add_slabs(strand, waiting, total)
        return total

    def finish(strand, last, total, eq, cols):
        first = strand == 0
        cos, sin = rope[strand]
        scalars = jnp.stack([slab_at[-1], my_row])
        made = [
            finish_kv(
                part,
                cols,
                last,
                scalars,
                key_weight,
                value_weight,
                total[1],
                total[2],
                cos,
                sin,
                [embed, total[4], total[5]] if first else None,
            )
            for part in range(width // cols)
        ]
        query = finish_q(
            min(2 * HEAD_DIM, width),
            last,
            scalars,
            query_weight,
            total[0],
            cos,
            sin,
            code_sets[strand][0],
            total[3] if first else eq,
            embed if first else None,
        )
        return made, query

    def spread_out(own, far):
        local = [own] + far
        return local + ctx_swap(local)

    def attend_part(strand, part, cols, blocks, query, tables, before, ids):
        return attend(
            strand == 0,
            part * cols,
            cols,
            ids,
            query[0],
            query[1],
            tables,
            *code_sets[strand],
            *rope[strand],
            blocks,
            before,
        )

    arrived, partial = [[], []], []
    cut = own_chains(tie(hidden, moving), 1)
    total = run_ring(0, moving, [None, (code_sets, cut)])
    last = arrived[0][-1]
    moving = hop([tie(block, item, total) for block, item in zip(cut, last)])
    made, query = finish(0, last, total, None, width)
    own, tables, eq = made[0][0], made[0][1:], query[2]
    far = ctx_far(own)

    total = run_ring(1, moving, [])
    blocks = spread_out(own, tie(far, partial[:1]))
    before = attend_part(0, 0, width, blocks, query, tables, None, tie(ids, total))
    last = tie(arrived[1][-1], before)

    lanes = lax.axis_size("groups") * ctx
    piece_rows = width // lanes
    lane = lax.axis_index("groups") * ctx + me
    piece = lax.dynamic_slice_in_dim(out_weight, lane * piece_rows, piece_rows, 0)
    pieces = []
    for shift in range(slabs):
        target = (head + shift) % slabs
        pieces.append(lax.dynamic_slice_in_dim(piece, target * tile, tile, 1))
    pieces = tie(pieces, arrived[1][max(0, slabs - 3)])

    def around(item, shift):
        return lax.ppermute(item, "head", [(i, (i + shift) % slabs) for i in range(slabs)])

    pieces = [around(tie(item, last), shift) if shift else item for shift, item in enumerate(pieces)]

    made, query_then = finish(1, last, total, eq, cols)
    own_then = [item[0] for item in made]
    far_then = [ctx_far(item) for item in own_then]
    far_then[0] = tie(far_then[0], own_then, query_then)
    pieces = tie(jnp.stack(pieces), far_then[0])
    out_slabs = lax.all_gather(pieces, ("groups", "ctx"), axis=1, tiled=True)
    combined, result = [], None
    for part in range(parts):
        blocks = spread_out(own_then[part], tie(far_then[part], combined))
        item = attend_part(1, part, cols, blocks, query_then, tables, before, ids)
        combined.append(item)
    for part, item in enumerate(combined):
        slab_rows = [around(item, shift) if shift else item for shift in range(slabs)]
        result = out_project(part, slab_rows, out_slabs, part == parts - 1, result)
    return result


def solution(mesh):
    return jax.shard_map(
        shards,
        mesh=mesh,
        in_specs=(
            P(None, ("groups", "ctx"), "head"),
            P(("groups", "ctx")),
            P("groups"),
            P("groups"),
            P(),
            P(None, "head"),
            P(None, "head"),
            P(None, "head"),
            P("head", None),
        ),
        out_specs=P(("groups", "ctx"), "head"),
        check_vma=False,
    )
```

```python
import functools
import math

import jax
import jax.numpy as jnp
from jax import lax
from jax.experimental import pallas as pl
from jax.experimental.pallas import tpu as pltpu
from jax.sharding import PartitionSpec as P

HEAD_DIM = 128
BASES = 4
CODES = 16
SUM_CODE = 8
ROPE_BASE = 10000.0
NEG_FILL = -1e30
COST_CUT = 64
SCORE_SCALE = math.log2(math.e) / math.sqrt(HEAD_DIM)
VMEM_LIMIT = 24 * 1024 * 1024
WEIGHT_VMEM_LIMIT = 50 * 1024 * 1024
F32 = jnp.float32
BF16 = jnp.bfloat16


def params(limit=VMEM_LIMIT):
    return pltpu.CompilerParams(vmem_limit_bytes=limit)


def cost(flops, moved, exps=0):
    return pl.CostEstimate(
        flops=flops // COST_CUT, bytes_accessed=moved // COST_CUT, transcendentals=exps // COST_CUT
    )


def dot(left, right):
    return jnp.dot(left, right, preferred_element_type=F32)


def rope_tables(positions):
    half = HEAD_DIM // 2
    freq = jnp.power(ROPE_BASE, -jnp.arange(half, dtype=F32) * 2.0 / HEAD_DIM)
    angle = positions[:, None] * freq[None, :]
    cos, sin = jnp.cos(angle), jnp.sin(angle)
    return jnp.concatenate([cos, cos], axis=1), jnp.concatenate([-sin, sin], axis=1)


def swapped(value):
    return pltpu.roll(value, HEAD_DIM // 2, axis=1)


def turned(value, cos, sin):
    return value * cos + swapped(value) * sin


def code_table(rows):
    high = rows.astype(BF16)
    low = (rows - high.astype(F32)).astype(BF16)
    at = lax.broadcasted_iota(jnp.int32, rows.shape, 0)
    return jnp.where(at < BASES, high.astype(F32), low.astype(F32)).astype(BF16)


def read_rows(refs, strand):
    parts = [ref[strand] if len(ref.shape) == 3 else ref[...] for ref in refs]
    return parts[0] if len(parts) == 1 else jnp.concatenate(parts, axis=0)


def local_call(kernel, name, scalars, operands, far, out_shape, scratch, work):
    vmem = pl.BlockSpec(memory_space=pltpu.VMEM)
    hbm = pl.BlockSpec(memory_space=pltpu.HBM)
    return pl.pallas_call(
        kernel,
        in_specs=[pl.BlockSpec(memory_space=pltpu.SMEM)]
        + [hbm] * far
        + [vmem] * (len(operands) - far),
        out_specs=[vmem] * len(out_shape),
        out_shape=out_shape,
        scratch_shapes=scratch,
        compiler_params=params(WEIGHT_VMEM_LIMIT),
        cost_estimate=work,
        name=name,
    )(scalars, *operands)


def fetch(weight_refs, slab, held, sems):
    tile = held.shape[1]
    copies = []
    for index, weight in enumerate(weight_refs):
        first = pl.multiple_of(slab * tile, tile)
        copy = pltpu.make_async_copy(
            weight.at[pl.ds(first, tile), :], held.at[index], sems.at[index]
        )
        copy.start()
        copies.append(copy)
    return copies


def slab_kernel(strand, slab_parts, with_embed, has_total, slab_ref, *refs):
    weights, refs = refs[:3], refs[3:]
    count = len(slab_parts)
    held, sems = refs[-2:]
    refs = refs[:-2]
    copies = [fetch(weights, slab_ref[at], held.at[at], sems.at[at]) for at in range(count)]
    if with_embed:
        embed_ref, refs = refs[0], refs[1:]
    rows = []
    for parts in slab_parts:
        rows.append(read_rows(refs[:parts], strand))
        refs = refs[parts:]
    size = 6 if with_embed else 3
    totals = refs[:size] if has_total else [None] * size
    outs = refs[-size:]
    tile = held.shape[2]
    for at in range(count):
        for index in range(3):
            copies[at][index].wait()
            weight = held[at, index]
            pairs = [(index, rows[at])]
            if with_embed:
                first = pl.multiple_of(slab_ref[at] * tile, tile)
                pairs.append((3 + index, embed_ref[:, pl.ds(first, tile)]))
            for slot, left in pairs:
                item = dot(left, weight)
                if at:
                    item = outs[slot][...] + item
                elif has_total:
                    item = totals[slot][...] + item
                outs[slot][...] = item


def slab_sums(slabs, scalars, strand, weights, embed=None, total=None):
    width = weights[0].shape[1]
    tile = slabs[0][0].shape[-1]
    rows = sum(x.shape[-2] for x in slabs[0])
    operands = [*weights] + ([embed] if embed is not None else [])
    for parts in slabs:
        operands += parts
    if total is not None:
        operands += total
    heights = [rows] * 3 + ([CODES] * 3 if embed is not None else [])
    return local_call(
        functools.partial(
            slab_kernel,
            strand,
            [len(parts) for parts in slabs],
            embed is not None,
            total is not None,
        ),
        "slab_sums",
        scalars,
        operands,
        3,
        [jax.ShapeDtypeStruct((height, width), F32) for height in heights],
        [
            pltpu.VMEM((len(slabs), 3, tile, width), BF16),
            pltpu.SemaphoreType.DMA((len(slabs), 3)),
        ],
        cost(6 * rows * tile * width * len(slabs), 6 * tile * width * len(slabs)),
    )


def finish_kv_kernel(x_count, part_count, with_embed, scalars, *refs):
    weights, refs = refs[:2], refs[2:]
    held, sems = refs[-2:]
    copies = fetch(weights, scalars[0], held, sems)
    x_refs, refs = refs[:x_count], refs[x_count:]
    (ksum_ref, vsum_ref, cos_ref, sin_ref), refs = refs[:4], refs[4:]
    if with_embed:
        (embed_ref, ek_ref, ev_ref), refs = refs[:3], refs[3:]
    kv_refs, refs = refs[:part_count], refs[part_count:]
    tile = held.shape[1]
    rows = read_rows(x_refs, 0)
    height, width = ksum_ref.shape
    part_cols = width // part_count
    own = pl.ds(pl.multiple_of(scalars[1] * height, height), height)
    cos, sin = cos_ref[own, :], sin_ref[own, :]
    if with_embed:
        embed = embed_ref[:, pl.ds(pl.multiple_of(scalars[0] * tile, tile), tile)]
        table_ref, swapped_ref, ev_out = refs[:3]
    copies[0].wait()
    key = ksum_ref[...] + dot(rows, held[0])
    for start in range(0, width, HEAD_DIM):
        part, at = start // part_cols, start % part_cols
        turned_key = turned(key[:, start : start + HEAD_DIM], cos, sin)
        kv_refs[part][0, :, at : at + HEAD_DIM] = turned_key.astype(BF16)
    if with_embed:
        ek = ek_ref[...] + dot(embed, held[0])
        table_ref[...] = code_table(ek)
        for start in range(0, width, HEAD_DIM):
            cols = slice(start, start + HEAD_DIM)
            swapped_ref[:, cols] = code_table(swapped(ek[:, cols]))
    copies[1].wait()
    value = vsum_ref[...] + dot(rows, held[1])
    for part in range(part_count):
        kv_refs[part][1] = value[:, part * part_cols : (part + 1) * part_cols].astype(BF16)
    if with_embed:
        ev_out[...] = ev_ref[...] + dot(embed, held[1])


def finish_kv(part_count, x_parts, scalars, wk, wv, ksum, vsum, cos, sin, embed_parts):
    tile = x_parts[0].shape[-1]
    rows, width = ksum.shape
    operands = [wk, wv, *x_parts, ksum, vsum, cos, sin]
    out_shape = [jax.ShapeDtypeStruct((2, rows, width // part_count), BF16)] * part_count
    if embed_parts is not None:
        operands += embed_parts
        out_shape += [jax.ShapeDtypeStruct((CODES, width), kind) for kind in (BF16, BF16, F32)]
    return local_call(
        functools.partial(finish_kv_kernel, len(x_parts), part_count, embed_parts is not None),
        "finish_kv",
        scalars,
        operands,
        2,
        out_shape,
        [pltpu.VMEM((2, tile, width), BF16), pltpu.SemaphoreType.DMA((2,))],
        cost(4 * rows * tile * width, 4 * tile * width + 14 * rows * width),
    )


def finish_q_kernel(x_count, with_embed, scalars, *refs):
    weights, refs = refs[:1], refs[1:]
    held, sems = refs[-2:]
    copies = fetch(weights, scalars[0], held, sems)
    x_refs, refs = refs[:x_count], refs[x_count:]
    (qsum_ref, cos_ref, sin_ref, codes_ref, eq_ref), refs = refs[:5], refs[5:]
    tile = held.shape[1]
    height, width = qsum_ref.shape
    own = pl.ds(pl.multiple_of(scalars[1] * height, height), height)
    cos, sin = cos_ref[own, :] * SCORE_SCALE, sin_ref[own, :] * SCORE_SCALE
    rows = read_rows(x_refs, 0)
    copies[0].wait()
    eq = eq_ref[...]
    if with_embed:
        embed_ref, q_ref, qm_ref, eq_out = refs[:4]
        first = pl.multiple_of(scalars[0] * tile, tile)
        eq = eq + dot(embed_ref[:, pl.ds(first, tile)], held[0])
        eq_out[...] = eq
    else:
        q_ref, qm_ref = refs[:2]
    query = qsum_ref[...] + dot(rows, held[0])
    mutant = query + dot(codes_ref[0], code_table(eq))
    for start in range(0, width, HEAD_DIM):
        cols = slice(start, start + HEAD_DIM)
        q_ref[:, cols] = turned(query[:, cols], cos, sin).astype(BF16)
        qm_ref[:, cols] = turned(mutant[:, cols], cos, sin).astype(BF16)


def finish_q(x_parts, scalars, wq, qsum, cos, sin, codes, eq, embed):
    tile = x_parts[0].shape[-1]
    rows, width = qsum.shape
    operands = [wq, *x_parts, qsum, cos, sin, codes, eq]
    out_shape = [jax.ShapeDtypeStruct((rows, width), BF16)] * 2
    if embed is not None:
        operands.append(embed)
        out_shape.append(jax.ShapeDtypeStruct((CODES, width), F32))
    return local_call(
        functools.partial(finish_q_kernel, len(x_parts), embed is not None),
        "finish_q",
        scalars,
        operands,
        1,
        out_shape,
        [pltpu.VMEM((1, tile, width), BF16), pltpu.SemaphoreType.DMA((1,))],
        cost(2 * rows * tile * width, 2 * tile * width + 8 * rows * width),
    )


def attend_kernel(forward, block_count, has_before, q_start, table_start, before_start, *refs):
    (ids_ref, q_ref, qm_ref, table_ref, swapped_ref, ev_ref), refs = refs[:6], refs[6:]
    (codes_ref, codes_t_ref, cos_ref, sin_ref), refs = refs[:4], refs[4:]
    kv_refs, refs = refs[:block_count], refs[block_count:]
    before_ref = None
    if has_before:
        before_ref, refs = refs[0], refs[1:]
    out_ref, top, acc = refs
    rows, cols_here = out_ref.shape
    heads = cols_here // HEAD_DIM
    tall = HEAD_DIM + CODES
    my_id = ids_ref[0]

    def block(index):
        kv_ref = kv_refs[index]
        first = pl.multiple_of(ids_ref[index] * rows, rows)
        cos = cos_ref[pl.ds(first, rows), :]
        sin = sin_ref[pl.ds(first, rows), :]
        codes, codes_t = codes_ref[index], codes_t_ref[index]
        here = slice(table_start, table_start + cols_here)
        change = dot(codes, table_ref[:, here])
        change_swapped = dot(codes, swapped_ref[:, here])
        if index == 0:
            key_at = lax.broadcasted_iota(jnp.int32, (rows, rows), 0)
            query_at = lax.broadcasted_iota(jnp.int32, (rows, rows), 1)
            seen = key_at <= query_at if forward else key_at >= query_at
        scores, values = [], []
        for head in range(heads):
            cols = slice(head * HEAD_DIM, (head + 1) * HEAD_DIM)
            q_cols = slice(q_start + cols.start, q_start + cols.stop)
            key = kv_ref[0, :, cols]
            mutant_key = (
                key.astype(F32) + change[:, cols] * cos + change_swapped[:, cols] * sin
            ).astype(BF16)
            values.append(jnp.concatenate([kv_ref[1, :, cols].T, codes_t], axis=0))
            for query, keys in ((q_ref[:, q_cols], key), (qm_ref[:, q_cols], mutant_key)):
                scores.append(
                    lax.dot_general(
                        keys, query, (((1,), (1,)), ((), ())), preferred_element_type=F32
                    )
                )
        fades, weights = [], []
        for unit, score in enumerate(scores):
            if index == 0:
                score = jnp.where(seen, score, NEG_FILL)
            peak = jnp.max(score, axis=0, keepdims=True)
            if index:
                old_peak = top[unit : unit + 1, :]
                peak = jnp.maximum(old_peak, peak)
                fades.append(jnp.exp2(old_peak - peak))
            top[unit : unit + 1, :] = peak
            weights.append(jnp.exp2(score - peak).astype(BF16))
        for unit, weight in enumerate(weights):
            area = slice(unit * tall, (unit + 1) * tall)
            product = dot(values[unit // 2], weight)
            acc[area, :] = acc[area, :] * fades[unit] + product if index else product

    for index in range(block_count):
        if index == 0:
            block(0)
        else:
            other = ids_ref[index]
            pl.when(other < my_id if forward else other > my_id)(functools.partial(block, index))

    code_at = lax.broadcasted_iota(jnp.int32, (CODES, HEAD_DIM), 0)
    for head in range(heads):
        cols = slice(head * HEAD_DIM, (head + 1) * HEAD_DIM)
        table_cols = slice(table_start + cols.start, table_start + cols.stop)
        ev = jnp.where(code_at < BASES, ev_ref[:, table_cols], 0.0)
        parts = []
        for kind in range(2):
            start = (2 * head + kind) * tall
            value = acc[start : start + HEAD_DIM, :]
            tail = acc[start + HEAD_DIM : start + tall, :]
            if kind:
                value = value + lax.dot_general(
                    ev,
                    tail,
                    (((0,), (0,)), ((), ())),
                    precision=lax.Precision.HIGHEST,
                    preferred_element_type=F32,
                )
            parts.append(value / tail[SUM_CODE : SUM_CODE + 1, :])
        difference = (parts[0] - parts[1]).T
        if has_before:
            earlier = before_ref[:, before_start + cols.start : before_start + cols.stop]
            out_ref[:, cols] = (0.5 * (earlier + difference)).astype(BF16)
        else:
            out_ref[:, cols] = difference


def attend(forward, start, cols, ids, q, qm, tables, codes, codes_t, cos, sin, kv_blocks, before):
    rows = q.shape[0]
    heads = cols // HEAD_DIM
    vmem = pl.BlockSpec(memory_space=pltpu.VMEM)
    operands = [q, qm, *tables, codes, codes_t, cos, sin, *kv_blocks]
    if before is not None:
        operands.append(before)
    count = len(kv_blocks)
    return pl.pallas_call(
        functools.partial(
            attend_kernel, forward, count, before is not None, start, start, start
        ),
        in_specs=[pl.BlockSpec(memory_space=pltpu.SMEM)] + [vmem] * len(operands),
        out_specs=vmem,
        out_shape=jax.ShapeDtypeStruct((rows, cols), F32 if before is None else BF16),
        scratch_shapes=[
            pltpu.VMEM((max(2 * heads, 8), rows), F32),
            pltpu.VMEM((2 * heads * (HEAD_DIM + CODES), rows), F32),
        ],
        compiler_params=params(),
        cost_estimate=cost(
            8 * rows * rows * count * cols,
            4 * count * rows * cols,
            2 * rows * rows * count * heads,
        ),
        name="attend_forward" if forward else "attend_reverse",
    )(ids, *operands)


def out_kernel(part, slabs, has_before, scalars, weight_ref, *refs):
    del scalars
    held, sems = refs[-2:]
    out_ref = refs[-3]
    row_refs = refs[:slabs]
    cols = held.shape[1]
    copies = []
    for index in range(slabs):
        copy = pltpu.make_async_copy(
            weight_ref.at[index, pl.ds(part * cols, cols), :], held.at[index], sems.at[index]
        )
        copy.start()
        copies.append(copy)
    total = refs[slabs][...] if has_before else None
    for index in range(slabs):
        copies[index].wait()
        item = dot(row_refs[index][...], held[index])
        total = item if total is None else total + item
    out_ref[...] = total.astype(out_ref.dtype)


def out_project(part, slab_rows, weight, last, before, scalars):
    slabs = len(slab_rows)
    rows, cols = slab_rows[0].shape
    width = weight.shape[2]
    operands = [weight, *slab_rows] + ([before] if before is not None else [])
    return local_call(
        functools.partial(out_kernel, part, slabs, before is not None),
        "out_project",
        scalars,
        operands,
        1,
        [jax.ShapeDtypeStruct((rows, width), BF16 if last else F32)],
        [pltpu.VMEM((slabs, cols, width), BF16), pltpu.SemaphoreType.DMA((slabs,))],
        cost(2 * slabs * rows * cols * width, 2 * slabs * cols * width),
    )[0]


def shards(
    hidden,
    strand_bases,
    variant_sites,
    base_shift,
    base_embed,
    query_weight,
    key_weight,
    value_weight,
    out_weight,
):
    rows, tile = hidden.shape[1:]
    ctx = lax.axis_size("ctx")
    slabs = lax.axis_size("head")
    me = lax.axis_index("ctx")
    head = lax.axis_index("head")
    window = rows * ctx
    width = query_weight.shape[1]
    cores = 2 if ctx % 2 == 0 else 1
    chains = 2 if rows % 32 == 0 else 1
    parts = 2 if width % (2 * HEAD_DIM) == 0 else 1
    cols = width // parts
    weights = (query_weight, key_weight, value_weight)
    my_row = me.astype(jnp.int32)
    ring = [(i, (i + 1) % slabs) for i in range(slabs)]
    slab_at = [((head - step) % slabs).astype(jnp.int32) for step in range(slabs)]

    def tie(items, *first):
        return lax.optimization_barrier((items, first))[0]

    def ctx_far(block):
        return [
            lax.ppermute(block, "ctx", [(i, (i + cores * shift) % ctx) for i in range(ctx)])
            for shift in range(1, ctx // cores)
        ]

    def ctx_swap(blocks):
        if cores == 1:
            return []
        return [lax.ppermute(item, "ctx", [(i, i ^ 1) for i in range(ctx)]) for item in blocks]

    def hop(blocks):
        return [lax.ppermute(block, "head", ring) for block in blocks]

    near = [(me - cores * shift) % ctx for shift in range(ctx // cores)]
    if cores == 2:
        near = near + [item ^ 1 for item in near]
    ids = jnp.stack(near).astype(jnp.int32)

    span = rows // chains

    def own_chains(source, strand):
        return [source[strand, chain * span : (chain + 1) * span] for chain in range(chains)]

    moving = hop(own_chains(hidden, 0))

    bases = [strand_bases] + ctx_far(strand_bases)
    bases = jnp.stack(bases + ctx_swap(bases))
    positions = ids[:, None] * rows + jnp.arange(rows, dtype=jnp.int32)[None, :]
    match = positions[:, :, None] == variant_sites[None, None, :]
    shifts = jnp.sum(jnp.where(match, base_shift[None, None, :], 0), axis=2)
    fresh = jnp.mod(bases + shifts, BASES)
    code_iota = jnp.arange(CODES, dtype=jnp.int32)

    def code_arrays(forward):
        want = code_iota % BASES
        want = want if forward else BASES - 1 - want

        def fill(old, new, want, at):
            codes = (new == want).astype(F32) - (old == want).astype(F32)
            codes = jnp.where(at < 2 * BASES, codes, (at == SUM_CODE).astype(F32))
            return codes.astype(BF16)

        return (
            fill(bases[:, :, None], fresh[:, :, None], want, code_iota),
            fill(bases[:, None, :], fresh[:, None, :], want[:, None], code_iota[:, None]),
        )

    embed = jnp.concatenate(
        [base_embed, base_embed, jnp.zeros((CODES - 2 * BASES, base_embed.shape[1]), BF16)]
    )
    window_iota = jnp.arange(window, dtype=jnp.int32)
    rope = [
        rope_tables(window_iota.astype(F32)),
        rope_tables((window - 1 - window_iota).astype(F32)),
    ]

    code_sets = [code_arrays(True), code_arrays(False)]

    def add_slabs(strand, steps, total):
        return slab_sums(
            [[hidden] if step == 0 else arrived[strand][step - 1] for step in steps],
            jnp.stack([slab_at[step] for step in steps]),
            strand,
            weights,
            embed if strand == 0 else None,
            total,
        )

    def run_ring(strand, moving, early):
        total, waiting = None, [0]
        partial.clear()
        for step in range(1, slabs):
            arrived[strand].append(moving)
            if step < slabs - 1:
                first = (early.pop(0) if early else None, total)
                moving = hop([tie(block, first) for block in moving])
                waiting.append(step)
                total = add_slabs(strand, waiting, total)
                partial.append(total)
                waiting = []
        if waiting:
            total = add_slabs(strand, waiting, total)
        return total

    def finish(strand, last, total, eq, count):
        first = strand == 0
        cos, sin = rope[strand]
        scalars = jnp.stack([slab_at[-1], my_row])
        made = finish_kv(
            count,
            last,
            scalars,
            key_weight,
            value_weight,
            total[1],
            total[2],
            cos,
            sin,
            [embed, total[4], total[5]] if first else None,
        )
        query = finish_q(
            last,
            scalars,
            query_weight,
            total[0],
            cos,
            sin,
            code_sets[strand][0],
            total[3] if first else eq,
            embed if first else None,
        )
        return made, query

    def spread_out(own, far):
        local = [own] + far
        return local + ctx_swap(local)

    def attend_part(strand, part, cols, blocks, query, tables, before, ids):
        return attend(
            strand == 0,
            part * cols,
            cols,
            ids,
            query[0],
            query[1],
            tables,
            *code_sets[strand],
            *rope[strand],
            blocks,
            before,
        )

    arrived, partial = [[], []], []
    cut = own_chains(tie(hidden, moving), 1)
    total = run_ring(0, moving, [None, (code_sets, cut)])
    last = arrived[0][-1]
    moving = hop([tie(block, item, total) for block, item in zip(cut, last)])
    made, query = finish(0, last, total, None, 1)
    own, tables, eq = made[0], made[1:], query[2]
    far = ctx_far(own)

    total = run_ring(1, moving, [(own,)])
    blocks = spread_out(own, tie(far, partial[:1]))
    before = attend_part(0, 0, width, blocks, query, tables, None, tie(ids, total))
    last = tie(arrived[1][-1], before)

    lanes = lax.axis_size("groups") * ctx
    piece_rows = width // lanes
    lane = lax.axis_index("groups") * ctx + me
    piece = lax.dynamic_slice_in_dim(out_weight, lane * piece_rows, piece_rows, 0)
    pieces = []
    for shift in range(slabs):
        target = (head + shift) % slabs
        pieces.append(lax.dynamic_slice_in_dim(piece, target * tile, tile, 1))
    pieces = tie(pieces, partial)

    def around(item, shift):
        return lax.ppermute(item, "head", [(i, (i + shift) % slabs) for i in range(slabs)])

    pieces = [around(tie(item, last), shift) if shift else item for shift, item in enumerate(pieces)]

    own_then, query_then = finish(1, last, total, eq, parts)
    far_then = [ctx_far(item) for item in own_then]
    far_then[0] = tie(far_then[0], own_then, query_then)
    pieces = tie(jnp.stack(pieces), far_then[0])
    out_slabs = lax.all_gather(pieces, ("groups", "ctx"), axis=1, tiled=True)
    combined, result = [], None
    for part in range(parts):
        blocks = spread_out(own_then[part], tie(far_then[part], combined))
        item = attend_part(1, part, cols, blocks, query_then, tables, before, ids)
        combined.append(item)
    for part, item in enumerate(combined):
        slab_rows = [around(item, shift) if shift else item for shift in range(slabs)]
        result = out_project(part, slab_rows, out_slabs, part == parts - 1, result, ids)
    return result


def solution(mesh):
    return jax.shard_map(
        shards,
        mesh=mesh,
        in_specs=(
            P(None, ("groups", "ctx"), "head"),
            P(("groups", "ctx")),
            P("groups"),
            P("groups"),
            P(),
            P(None, "head"),
            P(None, "head"),
            P(None, "head"),
            P("head", None),
        ),
        out_specs=P(("groups", "ctx"), "head"),
        check_vma=False,
    )
```

```python
import functools
import math

import jax
import jax.numpy as jnp
from jax import lax
from jax.experimental import pallas as pl
from jax.experimental.pallas import tpu as pltpu
from jax.sharding import PartitionSpec as P

HEAD_DIM = 128
BASES = 4
CODES = 16
SUM_CODE = 8
ROPE_BASE = 10000.0
NEG_FILL = -1e30
COST_CUT = 64
SCORE_SCALE = math.log2(math.e) / math.sqrt(HEAD_DIM)
VMEM_LIMIT = 24 * 1024 * 1024
WEIGHT_VMEM_LIMIT = 50 * 1024 * 1024
F32 = jnp.float32
BF16 = jnp.bfloat16


def params(limit=VMEM_LIMIT):
    return pltpu.CompilerParams(vmem_limit_bytes=limit)


def cost(flops, moved, exps=0):
    return pl.CostEstimate(
        flops=flops // COST_CUT, bytes_accessed=moved // COST_CUT, transcendentals=exps // COST_CUT
    )


def dot(left, right):
    return jnp.dot(left, right, preferred_element_type=F32)


def rope_tables(positions):
    half = HEAD_DIM // 2
    freq = jnp.power(ROPE_BASE, -jnp.arange(half, dtype=F32) * 2.0 / HEAD_DIM)
    angle = positions[:, None] * freq[None, :]
    cos, sin = jnp.cos(angle), jnp.sin(angle)
    return jnp.concatenate([cos, cos], axis=1), jnp.concatenate([-sin, sin], axis=1)


def swapped(value):
    return pltpu.roll(value, HEAD_DIM // 2, axis=1)


def turned(value, cos, sin):
    return value * cos + swapped(value) * sin


def code_table(rows):
    high = rows.astype(BF16)
    low = (rows - high.astype(F32)).astype(BF16)
    at = lax.broadcasted_iota(jnp.int32, rows.shape, 0)
    return jnp.where(at < BASES, high.astype(F32), low.astype(F32)).astype(BF16)


def read_rows(refs, strand):
    parts = [ref[strand] if len(ref.shape) == 3 else ref[...] for ref in refs]
    return parts[0] if len(parts) == 1 else jnp.concatenate(parts, axis=0)


def local_call(kernel, name, scalars, operands, far, out_shape, scratch, work):
    vmem = pl.BlockSpec(memory_space=pltpu.VMEM)
    hbm = pl.BlockSpec(memory_space=pltpu.HBM)
    return pl.pallas_call(
        kernel,
        in_specs=[pl.BlockSpec(memory_space=pltpu.SMEM)]
        + [hbm] * far
        + [vmem] * (len(operands) - far),
        out_specs=[vmem] * len(out_shape),
        out_shape=out_shape,
        scratch_shapes=scratch,
        compiler_params=params(WEIGHT_VMEM_LIMIT),
        cost_estimate=work,
        name=name,
    )(scalars, *operands)


def fetch(weight_refs, slab, held, sems):
    tile = held.shape[1]
    copies = []
    for index, weight in enumerate(weight_refs):
        first = pl.multiple_of(slab * tile, tile)
        copy = pltpu.make_async_copy(
            weight.at[pl.ds(first, tile), :], held.at[index], sems.at[index]
        )
        copy.start()
        copies.append(copy)
    return copies


def slab_kernel(strand, slab_parts, with_embed, has_total, slab_ref, *refs):
    weights, refs = refs[:3], refs[3:]
    count = len(slab_parts)
    held, sems = refs[-2:]
    refs = refs[:-2]
    copies = [fetch(weights, slab_ref[at], held.at[at], sems.at[at]) for at in range(count)]
    if with_embed:
        embed_ref, refs = refs[0], refs[1:]
    rows = []
    for parts in slab_parts:
        rows.append(read_rows(refs[:parts], strand))
        refs = refs[parts:]
    size = 6 if with_embed else 3
    totals = refs[:size] if has_total else [None] * size
    outs = refs[-size:]
    tile = held.shape[2]
    for at in range(count):
        for index in range(3):
            copies[at][index].wait()
            weight = held[at, index]
            pairs = [(index, rows[at])]
            if with_embed:
                first = pl.multiple_of(slab_ref[at] * tile, tile)
                pairs.append((3 + index, embed_ref[:, pl.ds(first, tile)]))
            for slot, left in pairs:
                item = dot(left, weight)
                if at:
                    item = outs[slot][...] + item
                elif has_total:
                    item = totals[slot][...] + item
                outs[slot][...] = item


def slab_sums(slabs, scalars, strand, weights, embed=None, total=None):
    width = weights[0].shape[1]
    tile = slabs[0][0].shape[-1]
    rows = sum(x.shape[-2] for x in slabs[0])
    operands = [*weights] + ([embed] if embed is not None else [])
    for parts in slabs:
        operands += parts
    if total is not None:
        operands += total
    heights = [rows] * 3 + ([CODES] * 3 if embed is not None else [])
    return local_call(
        functools.partial(
            slab_kernel,
            strand,
            [len(parts) for parts in slabs],
            embed is not None,
            total is not None,
        ),
        "slab_sums",
        scalars,
        operands,
        3,
        [jax.ShapeDtypeStruct((height, width), F32) for height in heights],
        [
            pltpu.VMEM((len(slabs), 3, tile, width), BF16),
            pltpu.SemaphoreType.DMA((len(slabs), 3)),
        ],
        cost(6 * rows * tile * width * len(slabs), 6 * tile * width * len(slabs)),
    )


def finish_kv_kernel(x_count, part_count, with_embed, scalars, *refs):
    weights, refs = refs[:2], refs[2:]
    held, sems = refs[-2:]
    copies = fetch(weights, scalars[0], held, sems)
    x_refs, refs = refs[:x_count], refs[x_count:]
    (ksum_ref, vsum_ref, cos_ref, sin_ref), refs = refs[:4], refs[4:]
    if with_embed:
        (embed_ref, ek_ref, ev_ref), refs = refs[:3], refs[3:]
    kv_refs, refs = refs[:part_count], refs[part_count:]
    tile = held.shape[1]
    rows = read_rows(x_refs, 0)
    height, width = ksum_ref.shape
    part_cols = width // part_count
    own = pl.ds(pl.multiple_of(scalars[1] * height, height), height)
    cos, sin = cos_ref[own, :], sin_ref[own, :]
    if with_embed:
        embed = embed_ref[:, pl.ds(pl.multiple_of(scalars[0] * tile, tile), tile)]
        table_ref, swapped_ref, ev_out = refs[:3]
    copies[0].wait()
    key = ksum_ref[...] + dot(rows, held[0])
    for start in range(0, width, HEAD_DIM):
        part, at = start // part_cols, start % part_cols
        turned_key = turned(key[:, start : start + HEAD_DIM], cos, sin)
        kv_refs[part][0, :, at : at + HEAD_DIM] = turned_key.astype(BF16)
    if with_embed:
        ek = ek_ref[...] + dot(embed, held[0])
        table_ref[...] = code_table(ek)
        for start in range(0, width, HEAD_DIM):
            cols = slice(start, start + HEAD_DIM)
            swapped_ref[:, cols] = code_table(swapped(ek[:, cols]))
    copies[1].wait()
    value = vsum_ref[...] + dot(rows, held[1])
    for part in range(part_count):
        kv_refs[part][1] = value[:, part * part_cols : (part + 1) * part_cols].astype(BF16)
    if with_embed:
        ev_out[...] = ev_ref[...] + dot(embed, held[1])


def finish_kv(part_count, x_parts, scalars, wk, wv, ksum, vsum, cos, sin, embed_parts):
    tile = x_parts[0].shape[-1]
    rows, width = ksum.shape
    operands = [wk, wv, *x_parts, ksum, vsum, cos, sin]
    out_shape = [jax.ShapeDtypeStruct((2, rows, width // part_count), BF16)] * part_count
    if embed_parts is not None:
        operands += embed_parts
        out_shape += [jax.ShapeDtypeStruct((CODES, width), kind) for kind in (BF16, BF16, F32)]
    return local_call(
        functools.partial(finish_kv_kernel, len(x_parts), part_count, embed_parts is not None),
        "finish_kv",
        scalars,
        operands,
        2,
        out_shape,
        [pltpu.VMEM((2, tile, width), BF16), pltpu.SemaphoreType.DMA((2,))],
        cost(4 * rows * tile * width, 4 * tile * width + 14 * rows * width),
    )


def finish_q_kernel(x_count, with_embed, scalars, *refs):
    weights, refs = refs[:1], refs[1:]
    held, sems = refs[-2:]
    copies = fetch(weights, scalars[0], held, sems)
    x_refs, refs = refs[:x_count], refs[x_count:]
    (qsum_ref, cos_ref, sin_ref, codes_ref, eq_ref), refs = refs[:5], refs[5:]
    tile = held.shape[1]
    height, width = qsum_ref.shape
    own = pl.ds(pl.multiple_of(scalars[1] * height, height), height)
    cos, sin = cos_ref[own, :] * SCORE_SCALE, sin_ref[own, :] * SCORE_SCALE
    rows = read_rows(x_refs, 0)
    copies[0].wait()
    eq = eq_ref[...]
    if with_embed:
        embed_ref, q_ref, qm_ref, eq_out = refs[:4]
        first = pl.multiple_of(scalars[0] * tile, tile)
        eq = eq + dot(embed_ref[:, pl.ds(first, tile)], held[0])
        eq_out[...] = eq
    else:
        q_ref, qm_ref = refs[:2]
    query = qsum_ref[...] + dot(rows, held[0])
    mutant = query + dot(codes_ref[0], code_table(eq))
    for start in range(0, width, HEAD_DIM):
        cols = slice(start, start + HEAD_DIM)
        q_ref[:, cols] = turned(query[:, cols], cos, sin).astype(BF16)
        qm_ref[:, cols] = turned(mutant[:, cols], cos, sin).astype(BF16)


def finish_q(x_parts, scalars, wq, qsum, cos, sin, codes, eq, embed):
    tile = x_parts[0].shape[-1]
    rows, width = qsum.shape
    operands = [wq, *x_parts, qsum, cos, sin, codes, eq]
    out_shape = [jax.ShapeDtypeStruct((rows, width), BF16)] * 2
    if embed is not None:
        operands.append(embed)
        out_shape.append(jax.ShapeDtypeStruct((CODES, width), F32))
    return local_call(
        functools.partial(finish_q_kernel, len(x_parts), embed is not None),
        "finish_q",
        scalars,
        operands,
        1,
        out_shape,
        [pltpu.VMEM((1, tile, width), BF16), pltpu.SemaphoreType.DMA((1,))],
        cost(2 * rows * tile * width, 2 * tile * width + 8 * rows * width),
    )


def attend_kernel(forward, block_count, has_before, q_start, table_start, before_start, *refs):
    (ids_ref, q_ref, qm_ref, table_ref, swapped_ref, ev_ref), refs = refs[:6], refs[6:]
    (codes_ref, codes_t_ref, cos_ref, sin_ref), refs = refs[:4], refs[4:]
    kv_refs, refs = refs[:block_count], refs[block_count:]
    before_ref = None
    if has_before:
        before_ref, refs = refs[0], refs[1:]
    out_ref, top, acc = refs
    rows, cols_here = out_ref.shape
    heads = cols_here // HEAD_DIM
    tall = HEAD_DIM + CODES
    my_id = ids_ref[0]

    def block(index):
        kv_ref = kv_refs[index]
        first = pl.multiple_of(ids_ref[index] * rows, rows)
        cos = cos_ref[pl.ds(first, rows), :]
        sin = sin_ref[pl.ds(first, rows), :]
        codes, codes_t = codes_ref[index], codes_t_ref[index]
        here = slice(table_start, table_start + cols_here)
        change = dot(codes, table_ref[:, here])
        change_swapped = dot(codes, swapped_ref[:, here])
        if index == 0:
            key_at = lax.broadcasted_iota(jnp.int32, (rows, rows), 0)
            query_at = lax.broadcasted_iota(jnp.int32, (rows, rows), 1)
            seen = key_at <= query_at if forward else key_at >= query_at
        scores, values = [], []
        for head in range(heads):
            cols = slice(head * HEAD_DIM, (head + 1) * HEAD_DIM)
            q_cols = slice(q_start + cols.start, q_start + cols.stop)
            key = kv_ref[0, :, cols]
            mutant_key = (
                key.astype(F32) + change[:, cols] * cos + change_swapped[:, cols] * sin
            ).astype(BF16)
            values.append(jnp.concatenate([kv_ref[1, :, cols].T, codes_t], axis=0))
            for query, keys in ((q_ref[:, q_cols], key), (qm_ref[:, q_cols], mutant_key)):
                scores.append(
                    lax.dot_general(
                        keys, query, (((1,), (1,)), ((), ())), preferred_element_type=F32
                    )
                )
        fades, weights = [], []
        for unit, score in enumerate(scores):
            if index == 0:
                score = jnp.where(seen, score, NEG_FILL)
            peak = jnp.max(score, axis=0, keepdims=True)
            if index:
                old_peak = top[unit : unit + 1, :]
                peak = jnp.maximum(old_peak, peak)
                fades.append(jnp.exp2(old_peak - peak))
            top[unit : unit + 1, :] = peak
            weights.append(jnp.exp2(score - peak).astype(BF16))
        for unit, weight in enumerate(weights):
            area = slice(unit * tall, (unit + 1) * tall)
            product = dot(values[unit // 2], weight)
            acc[area, :] = acc[area, :] * fades[unit] + product if index else product

    for index in range(block_count):
        if index == 0:
            block(0)
        else:
            other = ids_ref[index]
            pl.when(other < my_id if forward else other > my_id)(functools.partial(block, index))

    code_at = lax.broadcasted_iota(jnp.int32, (CODES, HEAD_DIM), 0)
    for head in range(heads):
        cols = slice(head * HEAD_DIM, (head + 1) * HEAD_DIM)
        table_cols = slice(table_start + cols.start, table_start + cols.stop)
        ev = jnp.where(code_at < BASES, ev_ref[:, table_cols], 0.0)
        parts = []
        for kind in range(2):
            start = (2 * head + kind) * tall
            value = acc[start : start + HEAD_DIM, :]
            tail = acc[start + HEAD_DIM : start + tall, :]
            if kind:
                value = value + lax.dot_general(
                    ev,
                    tail,
                    (((0,), (0,)), ((), ())),
                    precision=lax.Precision.HIGHEST,
                    preferred_element_type=F32,
                )
            parts.append(value / tail[SUM_CODE : SUM_CODE + 1, :])
        difference = (parts[0] - parts[1]).T
        if has_before:
            earlier = before_ref[:, before_start + cols.start : before_start + cols.stop]
            out_ref[:, cols] = (0.5 * (earlier + difference)).astype(BF16)
        else:
            out_ref[:, cols] = difference


def attend(forward, start, cols, ids, q, qm, tables, codes, codes_t, cos, sin, kv_blocks, before):
    rows = q.shape[0]
    heads = cols // HEAD_DIM
    vmem = pl.BlockSpec(memory_space=pltpu.VMEM)
    operands = [q, qm, *tables, codes, codes_t, cos, sin, *kv_blocks]
    if before is not None:
        operands.append(before)
    count = len(kv_blocks)
    return pl.pallas_call(
        functools.partial(
            attend_kernel, forward, count, before is not None, start, start, start
        ),
        in_specs=[pl.BlockSpec(memory_space=pltpu.SMEM)] + [vmem] * len(operands),
        out_specs=vmem,
        out_shape=jax.ShapeDtypeStruct((rows, cols), F32 if before is None else BF16),
        scratch_shapes=[
            pltpu.VMEM((max(2 * heads, 8), rows), F32),
            pltpu.VMEM((2 * heads * (HEAD_DIM + CODES), rows), F32),
        ],
        compiler_params=params(),
        cost_estimate=cost(
            8 * rows * rows * count * cols,
            4 * count * rows * cols,
            2 * rows * rows * count * heads,
        ),
        name="attend_forward" if forward else "attend_reverse",
    )(ids, *operands)


def out_kernel(part, slabs, has_before, scalars, weight_ref, *refs):
    del scalars
    held, sems = refs[-2:]
    out_ref = refs[-3]
    row_refs = refs[:slabs]
    cols = held.shape[1]
    copies = []
    for index in range(slabs):
        copy = pltpu.make_async_copy(
            weight_ref.at[index, pl.ds(part * cols, cols), :], held.at[index], sems.at[index]
        )
        copy.start()
        copies.append(copy)
    total = refs[slabs][...] if has_before else None
    for index in range(slabs):
        copies[index].wait()
        item = dot(row_refs[index][...], held[index])
        total = item if total is None else total + item
    out_ref[...] = total.astype(out_ref.dtype)


def out_project(part, slab_rows, weight, last, before, scalars):
    slabs = len(slab_rows)
    rows, cols = slab_rows[0].shape
    width = weight.shape[2]
    operands = [weight, *slab_rows] + ([before] if before is not None else [])
    return local_call(
        functools.partial(out_kernel, part, slabs, before is not None),
        "out_project",
        scalars,
        operands,
        1,
        [jax.ShapeDtypeStruct((rows, width), BF16 if last else F32)],
        [pltpu.VMEM((slabs, cols, width), BF16), pltpu.SemaphoreType.DMA((slabs,))],
        cost(2 * slabs * rows * cols * width, 2 * slabs * cols * width),
    )[0]


def shards(
    hidden,
    strand_bases,
    variant_sites,
    base_shift,
    base_embed,
    query_weight,
    key_weight,
    value_weight,
    out_weight,
):
    rows, tile = hidden.shape[1:]
    ctx = lax.axis_size("ctx")
    slabs = lax.axis_size("head")
    me = lax.axis_index("ctx")
    head = lax.axis_index("head")
    window = rows * ctx
    width = query_weight.shape[1]
    cores = 2 if ctx % 2 == 0 else 1
    chains = 2 if rows % 32 == 0 else 1
    parts = 2 if width % (2 * HEAD_DIM) == 0 else 1
    cols = width // parts
    weights = (query_weight, key_weight, value_weight)
    my_row = me.astype(jnp.int32)
    ring = [(i, (i + 1) % slabs) for i in range(slabs)]
    slab_at = [((head - step) % slabs).astype(jnp.int32) for step in range(slabs)]

    def tie(items, *first):
        return lax.optimization_barrier((items, first))[0]

    def ctx_far(block):
        return [
            lax.ppermute(block, "ctx", [(i, (i + cores * shift) % ctx) for i in range(ctx)])
            for shift in range(1, ctx // cores)
        ]

    def ctx_swap(blocks):
        if cores == 1:
            return []
        return [lax.ppermute(item, "ctx", [(i, i ^ 1) for i in range(ctx)]) for item in blocks]

    def hop(blocks):
        return [lax.ppermute(block, "head", ring) for block in blocks]

    near = [(me - cores * shift) % ctx for shift in range(ctx // cores)]
    if cores == 2:
        near = near + [item ^ 1 for item in near]
    ids = jnp.stack(near).astype(jnp.int32)

    span = rows // chains

    def own_chains(source, strand):
        return [source[strand, chain * span : (chain + 1) * span] for chain in range(chains)]

    moving = hop(own_chains(hidden, 0))

    bases = [strand_bases] + ctx_far(strand_bases)
    bases = jnp.stack(bases + ctx_swap(bases))
    positions = ids[:, None] * rows + jnp.arange(rows, dtype=jnp.int32)[None, :]
    match = positions[:, :, None] == variant_sites[None, None, :]
    shifts = jnp.sum(jnp.where(match, base_shift[None, None, :], 0), axis=2)
    fresh = jnp.mod(bases + shifts, BASES)
    code_iota = jnp.arange(CODES, dtype=jnp.int32)

    def code_arrays(forward):
        want = code_iota % BASES
        want = want if forward else BASES - 1 - want

        def fill(old, new, want, at):
            codes = (new == want).astype(F32) - (old == want).astype(F32)
            codes = jnp.where(at < 2 * BASES, codes, (at == SUM_CODE).astype(F32))
            return codes.astype(BF16)

        return (
            fill(bases[:, :, None], fresh[:, :, None], want, code_iota),
            fill(bases[:, None, :], fresh[:, None, :], want[:, None], code_iota[:, None]),
        )

    embed = jnp.concatenate(
        [base_embed, base_embed, jnp.zeros((CODES - 2 * BASES, base_embed.shape[1]), BF16)]
    )
    window_iota = jnp.arange(window, dtype=jnp.int32)
    rope = [
        rope_tables(window_iota.astype(F32)),
        rope_tables((window - 1 - window_iota).astype(F32)),
    ]

    code_sets = [code_arrays(True), code_arrays(False)]

    def add_slabs(strand, steps, total):
        return slab_sums(
            [[hidden] if step == 0 else arrived[strand][step - 1] for step in steps],
            jnp.stack([slab_at[step] for step in steps]),
            strand,
            weights,
            embed if strand == 0 else None,
            total,
        )

    def run_ring(strand, moving, early):
        total, waiting = None, [0]
        partial.clear()
        for step in range(1, slabs):
            arrived[strand].append(moving)
            if step < slabs - 1:
                first = (early.pop(0) if early else None, total)
                moving = hop(moving[:-1] + [tie(moving[-1], first)])
                waiting.append(step)
                total = add_slabs(strand, waiting, total)
                partial.append(total)
                waiting = []
        if waiting:
            total = add_slabs(strand, waiting, total)
        return total

    def finish(strand, last, total, eq, count):
        first = strand == 0
        cos, sin = rope[strand]
        scalars = jnp.stack([slab_at[-1], my_row])
        made = finish_kv(
            count,
            last,
            scalars,
            key_weight,
            value_weight,
            total[1],
            total[2],
            cos,
            sin,
            [embed, total[4], total[5]] if first else None,
        )
        query = finish_q(
            last,
            scalars,
            query_weight,
            total[0],
            cos,
            sin,
            code_sets[strand][0],
            total[3] if first else eq,
            embed if first else None,
        )
        return made, query

    def spread_out(own, far):
        local = [own] + far
        return local + ctx_swap(local)

    def attend_part(strand, part, cols, blocks, query, tables, before, ids):
        return attend(
            strand == 0,
            part * cols,
            cols,
            ids,
            query[0],
            query[1],
            tables,
            *code_sets[strand],
            *rope[strand],
            blocks,
            before,
        )

    arrived, partial = [[], []], []
    cut = own_chains(tie(hidden, moving), 1)
    lanes = lax.axis_size("groups") * ctx
    piece_rows = width // lanes
    lane = lax.axis_index("groups") * ctx + me
    piece = lax.dynamic_slice_in_dim(out_weight, lane * piece_rows, piece_rows, 0)
    pieces = []
    for shift in range(slabs):
        target = (head + shift) % slabs
        pieces.append(lax.dynamic_slice_in_dim(piece, target * tile, tile, 1))
    def around(item, shift):
        return lax.ppermute(item, "head", [(i, (i + shift) % slabs) for i in range(slabs)])

    pieces = [around(tie(item, moving), shift) if shift else item for shift, item in enumerate(pieces)]
    total = run_ring(0, moving, [rope, (code_sets, cut, pieces)])
    last = arrived[0][-1]
    moving = [tie(block, item) for block, item in zip(cut, last)]
    moving = hop(moving[:-1] + [tie(moving[-1], total)])
    made, query = finish(0, last, total, None, 1)
    own, tables, eq = made[0], made[1:], query[2]
    far = ctx_far(own)

    total = run_ring(1, moving, [(own,)])
    blocks = spread_out(own, tie(far, arrived[1][0]))
    before = attend_part(0, 0, width, blocks, query, tables, None, tie(ids, total))
    last = tie(arrived[1][-1], before)

    own_then, query_then = finish(1, last, total, eq, parts)
    far_then = [ctx_far(item) for item in own_then]
    far_then[0] = tie(far_then[0], own_then, query_then)
    pieces = tie(jnp.stack(pieces), own)
    out_slabs = lax.all_gather(pieces, ("groups", "ctx"), axis=1, tiled=True)
    combined, result = [], None
    for part in range(parts):
        blocks = spread_out(own_then[part], tie(far_then[part], combined))
        item = attend_part(1, part, cols, blocks, query_then, tables, before, ids)
        combined.append(item)
    for part, item in enumerate(combined):
        slab_rows = [around(item, shift) if shift else item for shift in range(slabs)]
        result = out_project(part, slab_rows, out_slabs, part == parts - 1, result, ids)
    return result


def solution(mesh):
    return jax.shard_map(
        shards,
        mesh=mesh,
        in_specs=(
            P(None, ("groups", "ctx"), "head"),
            P(("groups", "ctx")),
            P("groups"),
            P("groups"),
            P(),
            P(None, "head"),
            P(None, "head"),
            P(None, "head"),
            P("head", None),
        ),
        out_specs=P(("groups", "ctx"), "head"),
        check_vma=False,
    )
```

```python
import functools
import math

import jax
import jax.numpy as jnp
from jax import lax
from jax.experimental import pallas as pl
from jax.experimental.pallas import tpu as pltpu
from jax.sharding import PartitionSpec as P

HEAD_DIM = 128
BASES = 4
CODES = 16
SUM_CODE = 8
ROPE_BASE = 10000.0
NEG_FILL = -1e30
COST_CUT = 64
SCORE_SCALE = math.log2(math.e) / math.sqrt(HEAD_DIM)
VMEM_LIMIT = 24 * 1024 * 1024
WEIGHT_VMEM_LIMIT = 50 * 1024 * 1024
F32 = jnp.float32
BF16 = jnp.bfloat16


def params(limit=VMEM_LIMIT):
    return pltpu.CompilerParams(vmem_limit_bytes=limit)


def cost(flops, moved, exps=0):
    return pl.CostEstimate(
        flops=flops // COST_CUT, bytes_accessed=moved // COST_CUT, transcendentals=exps // COST_CUT
    )


def dot(left, right):
    return jnp.dot(left, right, preferred_element_type=F32)


def rope_tables(positions):
    half = HEAD_DIM // 2
    freq = jnp.power(ROPE_BASE, -jnp.arange(half, dtype=F32) * 2.0 / HEAD_DIM)
    angle = positions[:, None] * freq[None, :]
    cos, sin = jnp.cos(angle), jnp.sin(angle)
    return jnp.concatenate([cos, cos], axis=1), jnp.concatenate([-sin, sin], axis=1)


def swapped(value):
    return pltpu.roll(value, HEAD_DIM // 2, axis=1)


def turned(value, cos, sin):
    return value * cos + swapped(value) * sin


def code_table(rows):
    high = rows.astype(BF16)
    low = (rows - high.astype(F32)).astype(BF16)
    at = lax.broadcasted_iota(jnp.int32, rows.shape, 0)
    return jnp.where(at < BASES, high.astype(F32), low.astype(F32)).astype(BF16)


def read_rows(refs, strand):
    parts = [ref[strand] if len(ref.shape) == 3 else ref[...] for ref in refs]
    return parts[0] if len(parts) == 1 else jnp.concatenate(parts, axis=0)


def local_call(kernel, name, scalars, operands, far, out_shape, scratch, work):
    vmem = pl.BlockSpec(memory_space=pltpu.VMEM)
    hbm = pl.BlockSpec(memory_space=pltpu.HBM)
    return pl.pallas_call(
        kernel,
        in_specs=[pl.BlockSpec(memory_space=pltpu.SMEM)]
        + [hbm] * far
        + [vmem] * (len(operands) - far),
        out_specs=[vmem] * len(out_shape),
        out_shape=out_shape,
        scratch_shapes=scratch,
        compiler_params=params(WEIGHT_VMEM_LIMIT),
        cost_estimate=work,
        name=name,
    )(scalars, *operands)


def fetch(weight_refs, slab, held, sems):
    tile = held.shape[1]
    copies = []
    for index, weight in enumerate(weight_refs):
        first = pl.multiple_of(slab * tile, tile)
        copy = pltpu.make_async_copy(
            weight.at[pl.ds(first, tile), :], held.at[index], sems.at[index]
        )
        copy.start()
        copies.append(copy)
    return copies


def slab_kernel(strand, slab_parts, with_embed, has_total, slab_ref, *refs):
    weights, refs = refs[:3], refs[3:]
    count = len(slab_parts)
    held, sems = refs[-2:]
    refs = refs[:-2]
    copies = [fetch(weights, slab_ref[at], held.at[at], sems.at[at]) for at in range(count)]
    if with_embed:
        embed_ref, refs = refs[0], refs[1:]
    rows = []
    for parts in slab_parts:
        rows.append(read_rows(refs[:parts], strand))
        refs = refs[parts:]
    size = 6 if with_embed else 3
    totals = refs[:size] if has_total else [None] * size
    outs = refs[-size:]
    tile = held.shape[2]
    for at in range(count):
        for index in range(3):
            copies[at][index].wait()
            weight = held[at, index]
            pairs = [(index, rows[at])]
            if with_embed:
                first = pl.multiple_of(slab_ref[at] * tile, tile)
                pairs.append((3 + index, embed_ref[:, pl.ds(first, tile)]))
            for slot, left in pairs:
                item = dot(left, weight)
                if at:
                    item = outs[slot][...] + item
                elif has_total:
                    item = totals[slot][...] + item
                outs[slot][...] = item


def slab_sums(slabs, scalars, strand, weights, embed=None, total=None):
    width = weights[0].shape[1]
    tile = slabs[0][0].shape[-1]
    rows = sum(x.shape[-2] for x in slabs[0])
    operands = [*weights] + ([embed] if embed is not None else [])
    for parts in slabs:
        operands += parts
    if total is not None:
        operands += total
    heights = [rows] * 3 + ([CODES] * 3 if embed is not None else [])
    return local_call(
        functools.partial(
            slab_kernel,
            strand,
            [len(parts) for parts in slabs],
            embed is not None,
            total is not None,
        ),
        "slab_sums",
        scalars,
        operands,
        3,
        [jax.ShapeDtypeStruct((height, width), F32) for height in heights],
        [
            pltpu.VMEM((len(slabs), 3, tile, width), BF16),
            pltpu.SemaphoreType.DMA((len(slabs), 3)),
        ],
        cost(6 * rows * tile * width * len(slabs), 6 * tile * width * len(slabs)),
    )


def finish_kv_kernel(x_count, part_count, with_embed, scalars, *refs):
    weights, refs = refs[:2], refs[2:]
    held, sems = refs[-2:]
    copies = fetch(weights, scalars[0], held, sems)
    x_refs, refs = refs[:x_count], refs[x_count:]
    (ksum_ref, vsum_ref, cos_ref, sin_ref), refs = refs[:4], refs[4:]
    if with_embed:
        (embed_ref, ek_ref, ev_ref), refs = refs[:3], refs[3:]
    kv_refs, refs = refs[:part_count], refs[part_count:]
    tile = held.shape[1]
    rows = read_rows(x_refs, 0)
    height, width = ksum_ref.shape
    part_cols = width // part_count
    own = pl.ds(pl.multiple_of(scalars[1] * height, height), height)
    cos, sin = cos_ref[own, :], sin_ref[own, :]
    if with_embed:
        embed = embed_ref[:, pl.ds(pl.multiple_of(scalars[0] * tile, tile), tile)]
        table_ref, swapped_ref, ev_out = refs[:3]
    copies[0].wait()
    key = ksum_ref[...] + dot(rows, held[0])
    for start in range(0, width, HEAD_DIM):
        part, at = start // part_cols, start % part_cols
        turned_key = turned(key[:, start : start + HEAD_DIM], cos, sin)
        kv_refs[part][0, :, at : at + HEAD_DIM] = turned_key.astype(BF16)
    if with_embed:
        ek = ek_ref[...] + dot(embed, held[0])
        table_ref[...] = code_table(ek)
        for start in range(0, width, HEAD_DIM):
            cols = slice(start, start + HEAD_DIM)
            swapped_ref[:, cols] = code_table(swapped(ek[:, cols]))
    copies[1].wait()
    value = vsum_ref[...] + dot(rows, held[1])
    for part in range(part_count):
        kv_refs[part][1] = value[:, part * part_cols : (part + 1) * part_cols].astype(BF16)
    if with_embed:
        ev_out[...] = ev_ref[...] + dot(embed, held[1])


def finish_kv(part_count, x_parts, scalars, wk, wv, ksum, vsum, cos, sin, embed_parts):
    tile = x_parts[0].shape[-1]
    rows, width = ksum.shape
    operands = [wk, wv, *x_parts, ksum, vsum, cos, sin]
    out_shape = [jax.ShapeDtypeStruct((2, rows, width // part_count), BF16)] * part_count
    if embed_parts is not None:
        operands += embed_parts
        out_shape += [jax.ShapeDtypeStruct((CODES, width), kind) for kind in (BF16, BF16, F32)]
    return local_call(
        functools.partial(finish_kv_kernel, len(x_parts), part_count, embed_parts is not None),
        "finish_kv",
        scalars,
        operands,
        2,
        out_shape,
        [pltpu.VMEM((2, tile, width), BF16), pltpu.SemaphoreType.DMA((2,))],
        cost(4 * rows * tile * width, 4 * tile * width + 14 * rows * width),
    )


def finish_q_kernel(x_count, with_embed, scalars, *refs):
    weights, refs = refs[:1], refs[1:]
    held, sems = refs[-2:]
    copies = fetch(weights, scalars[0], held, sems)
    x_refs, refs = refs[:x_count], refs[x_count:]
    (qsum_ref, cos_ref, sin_ref, codes_ref, eq_ref), refs = refs[:5], refs[5:]
    tile = held.shape[1]
    height, width = qsum_ref.shape
    own = pl.ds(pl.multiple_of(scalars[1] * height, height), height)
    cos, sin = cos_ref[own, :] * SCORE_SCALE, sin_ref[own, :] * SCORE_SCALE
    rows = read_rows(x_refs, 0)
    copies[0].wait()
    eq = eq_ref[...]
    if with_embed:
        embed_ref, q_ref, qm_ref, eq_out = refs[:4]
        first = pl.multiple_of(scalars[0] * tile, tile)
        eq = eq + dot(embed_ref[:, pl.ds(first, tile)], held[0])
        eq_out[...] = eq
    else:
        q_ref, qm_ref = refs[:2]
    query = qsum_ref[...] + dot(rows, held[0])
    mutant = query + dot(codes_ref[0], code_table(eq))
    for start in range(0, width, HEAD_DIM):
        cols = slice(start, start + HEAD_DIM)
        q_ref[:, cols] = turned(query[:, cols], cos, sin).astype(BF16)
        qm_ref[:, cols] = turned(mutant[:, cols], cos, sin).astype(BF16)


def finish_q(x_parts, scalars, wq, qsum, cos, sin, codes, eq, embed):
    tile = x_parts[0].shape[-1]
    rows, width = qsum.shape
    operands = [wq, *x_parts, qsum, cos, sin, codes, eq]
    out_shape = [jax.ShapeDtypeStruct((rows, width), BF16)] * 2
    if embed is not None:
        operands.append(embed)
        out_shape.append(jax.ShapeDtypeStruct((CODES, width), F32))
    return local_call(
        functools.partial(finish_q_kernel, len(x_parts), embed is not None),
        "finish_q",
        scalars,
        operands,
        1,
        out_shape,
        [pltpu.VMEM((1, tile, width), BF16), pltpu.SemaphoreType.DMA((1,))],
        cost(2 * rows * tile * width, 2 * tile * width + 8 * rows * width),
    )


def attend_kernel(forward, block_count, has_before, q_start, table_start, before_start, *refs):
    (ids_ref, q_ref, qm_ref, table_ref, swapped_ref, ev_ref), refs = refs[:6], refs[6:]
    (codes_ref, codes_t_ref, cos_ref, sin_ref), refs = refs[:4], refs[4:]
    kv_refs, refs = refs[:block_count], refs[block_count:]
    before_ref = None
    if has_before:
        before_ref, refs = refs[0], refs[1:]
    out_ref, top, acc = refs
    rows, cols_here = out_ref.shape
    heads = cols_here // HEAD_DIM
    tall = HEAD_DIM + CODES
    my_id = ids_ref[0]

    def block(index):
        kv_ref = kv_refs[index]
        first = pl.multiple_of(ids_ref[index] * rows, rows)
        cos = cos_ref[pl.ds(first, rows), :]
        sin = sin_ref[pl.ds(first, rows), :]
        codes, codes_t = codes_ref[index], codes_t_ref[index]
        here = slice(table_start, table_start + cols_here)
        change = dot(codes, table_ref[:, here])
        change_swapped = dot(codes, swapped_ref[:, here])
        if index == 0:
            key_at = lax.broadcasted_iota(jnp.int32, (rows, rows), 0)
            query_at = lax.broadcasted_iota(jnp.int32, (rows, rows), 1)
            seen = key_at <= query_at if forward else key_at >= query_at
        scores, values = [], []
        for head in range(heads):
            cols = slice(head * HEAD_DIM, (head + 1) * HEAD_DIM)
            q_cols = slice(q_start + cols.start, q_start + cols.stop)
            key = kv_ref[0, :, cols]
            mutant_key = (
                key.astype(F32) + change[:, cols] * cos + change_swapped[:, cols] * sin
            ).astype(BF16)
            values.append(jnp.concatenate([kv_ref[1, :, cols].T, codes_t], axis=0))
            for query, keys in ((q_ref[:, q_cols], key), (qm_ref[:, q_cols], mutant_key)):
                scores.append(
                    lax.dot_general(
                        keys, query, (((1,), (1,)), ((), ())), preferred_element_type=F32
                    )
                )
        fades, weights = [], []
        for unit, score in enumerate(scores):
            if index == 0:
                score = jnp.where(seen, score, NEG_FILL)
            peak = jnp.max(score, axis=0, keepdims=True)
            if index:
                old_peak = top[unit : unit + 1, :]
                peak = jnp.maximum(old_peak, peak)
                fades.append(jnp.exp2(old_peak - peak))
            top[unit : unit + 1, :] = peak
            weights.append(jnp.exp2(score - peak).astype(BF16))
        for unit, weight in enumerate(weights):
            area = slice(unit * tall, (unit + 1) * tall)
            product = dot(values[unit // 2], weight)
            acc[area, :] = acc[area, :] * fades[unit] + product if index else product

    for index in range(block_count):
        if index == 0:
            block(0)
        else:
            other = ids_ref[index]
            pl.when(other < my_id if forward else other > my_id)(functools.partial(block, index))

    code_at = lax.broadcasted_iota(jnp.int32, (CODES, HEAD_DIM), 0)
    for head in range(heads):
        cols = slice(head * HEAD_DIM, (head + 1) * HEAD_DIM)
        table_cols = slice(table_start + cols.start, table_start + cols.stop)
        ev = jnp.where(code_at < BASES, ev_ref[:, table_cols], 0.0)
        parts = []
        for kind in range(2):
            start = (2 * head + kind) * tall
            value = acc[start : start + HEAD_DIM, :]
            tail = acc[start + HEAD_DIM : start + tall, :]
            if kind:
                value = value + lax.dot_general(
                    ev,
                    tail,
                    (((0,), (0,)), ((), ())),
                    precision=lax.Precision.HIGHEST,
                    preferred_element_type=F32,
                )
            parts.append(value / tail[SUM_CODE : SUM_CODE + 1, :])
        difference = (parts[0] - parts[1]).T
        if has_before:
            earlier = before_ref[:, before_start + cols.start : before_start + cols.stop]
            out_ref[:, cols] = (0.5 * (earlier + difference)).astype(BF16)
        else:
            out_ref[:, cols] = difference


def attend(forward, start, cols, ids, q, qm, tables, codes, codes_t, cos, sin, kv_blocks, before):
    rows = q.shape[0]
    heads = cols // HEAD_DIM
    vmem = pl.BlockSpec(memory_space=pltpu.VMEM)
    operands = [q, qm, *tables, codes, codes_t, cos, sin, *kv_blocks]
    if before is not None:
        operands.append(before)
    count = len(kv_blocks)
    return pl.pallas_call(
        functools.partial(
            attend_kernel, forward, count, before is not None, start, start, start
        ),
        in_specs=[pl.BlockSpec(memory_space=pltpu.SMEM)] + [vmem] * len(operands),
        out_specs=vmem,
        out_shape=jax.ShapeDtypeStruct((rows, cols), F32 if before is None else BF16),
        scratch_shapes=[
            pltpu.VMEM((max(2 * heads, 8), rows), F32),
            pltpu.VMEM((2 * heads * (HEAD_DIM + CODES), rows), F32),
        ],
        compiler_params=params(),
        cost_estimate=cost(
            8 * rows * rows * count * cols,
            4 * count * rows * cols,
            2 * rows * rows * count * heads,
        ),
        name="attend_forward" if forward else "attend_reverse",
    )(ids, *operands)


def out_kernel(part, slabs, has_before, scalars, weight_ref, *refs):
    del scalars
    held, sems = refs[-2:]
    out_ref = refs[-3]
    row_refs = refs[:slabs]
    cols = held.shape[1]
    copies = []
    for index in range(slabs):
        copy = pltpu.make_async_copy(
            weight_ref.at[index, pl.ds(part * cols, cols), :], held.at[index], sems.at[index]
        )
        copy.start()
        copies.append(copy)
    total = refs[slabs][...] if has_before else None
    for index in range(slabs):
        copies[index].wait()
        item = dot(row_refs[index][...], held[index])
        total = item if total is None else total + item
    out_ref[...] = total.astype(out_ref.dtype)


def out_project(part, slab_rows, weight, last, before, scalars):
    slabs = len(slab_rows)
    rows, cols = slab_rows[0].shape
    width = weight.shape[2]
    operands = [weight, *slab_rows] + ([before] if before is not None else [])
    return local_call(
        functools.partial(out_kernel, part, slabs, before is not None),
        "out_project",
        scalars,
        operands,
        1,
        [jax.ShapeDtypeStruct((rows, width), BF16 if last else F32)],
        [pltpu.VMEM((slabs, cols, width), BF16), pltpu.SemaphoreType.DMA((slabs,))],
        cost(2 * slabs * rows * cols * width, 2 * slabs * cols * width),
    )[0]


def shards(
    hidden,
    strand_bases,
    variant_sites,
    base_shift,
    base_embed,
    query_weight,
    key_weight,
    value_weight,
    out_weight,
):
    rows, tile = hidden.shape[1:]
    ctx = lax.axis_size("ctx")
    slabs = lax.axis_size("head")
    me = lax.axis_index("ctx")
    head = lax.axis_index("head")
    window = rows * ctx
    width = query_weight.shape[1]
    cores = 2 if ctx % 2 == 0 else 1
    chains = 2 if rows % 32 == 0 else 1
    parts = 2 if width % (2 * HEAD_DIM) == 0 else 1
    cols = width // parts
    weights = (query_weight, key_weight, value_weight)
    my_row = me.astype(jnp.int32)
    ring = [(i, (i + 1) % slabs) for i in range(slabs)]
    slab_at = [((head - step) % slabs).astype(jnp.int32) for step in range(slabs)]

    def tie(items, *first):
        return lax.optimization_barrier((items, first))[0]

    def ctx_far(block):
        return [
            lax.ppermute(block, "ctx", [(i, (i + cores * shift) % ctx) for i in range(ctx)])
            for shift in range(1, ctx // cores)
        ]

    def ctx_swap(blocks):
        if cores == 1:
            return []
        return [lax.ppermute(item, "ctx", [(i, i ^ 1) for i in range(ctx)]) for item in blocks]

    def hop(blocks):
        return [lax.ppermute(block, "head", ring) for block in blocks]

    near = [(me - cores * shift) % ctx for shift in range(ctx // cores)]
    if cores == 2:
        near = near + [item ^ 1 for item in near]
    ids = jnp.stack(near).astype(jnp.int32)

    span = rows // chains

    def own_chains(source, strand):
        return [source[strand, chain * span : (chain + 1) * span] for chain in range(chains)]

    moving = hop(own_chains(hidden, 0))

    bases = [strand_bases] + ctx_far(strand_bases)
    bases = jnp.stack(bases + ctx_swap(bases))
    positions = ids[:, None] * rows + jnp.arange(rows, dtype=jnp.int32)[None, :]
    match = positions[:, :, None] == variant_sites[None, None, :]
    shifts = jnp.sum(jnp.where(match, base_shift[None, None, :], 0), axis=2)
    fresh = jnp.mod(bases + shifts, BASES)
    code_iota = jnp.arange(CODES, dtype=jnp.int32)

    def code_arrays(forward):
        want = code_iota % BASES
        want = want if forward else BASES - 1 - want

        def fill(old, new, want, at):
            codes = (new == want).astype(F32) - (old == want).astype(F32)
            codes = jnp.where(at < 2 * BASES, codes, (at == SUM_CODE).astype(F32))
            return codes.astype(BF16)

        return (
            fill(bases[:, :, None], fresh[:, :, None], want, code_iota),
            fill(bases[:, None, :], fresh[:, None, :], want[:, None], code_iota[:, None]),
        )

    embed = jnp.concatenate(
        [base_embed, base_embed, jnp.zeros((CODES - 2 * BASES, base_embed.shape[1]), BF16)]
    )
    window_iota = jnp.arange(window, dtype=jnp.int32)
    rope = [
        rope_tables(window_iota.astype(F32)),
        rope_tables((window - 1 - window_iota).astype(F32)),
    ]

    code_sets = [code_arrays(True), code_arrays(False)]

    def add_slabs(strand, steps, total):
        return slab_sums(
            [[hidden] if step == 0 else arrived[strand][step - 1] for step in steps],
            jnp.stack([slab_at[step] for step in steps]),
            strand,
            weights,
            embed if strand == 0 else None,
            total,
        )

    def run_ring(strand, moving, early):
        total, waiting = None, [0]
        partial.clear()
        for step in range(1, slabs):
            arrived[strand].append(moving)
            if step < slabs - 1:
                first = (early.pop(0) if early else None, total)
                moving = hop(moving[:-1] + [tie(moving[-1], first)])
                waiting.append(step)
                total = add_slabs(strand, waiting, total)
                partial.append(total)
                waiting = []
        if waiting:
            total = add_slabs(strand, waiting, total)
        return total

    def finish(strand, last, total, eq, count):
        first = strand == 0
        cos, sin = rope[strand]
        scalars = jnp.stack([slab_at[-1], my_row])
        made = finish_kv(
            count,
            last,
            scalars,
            key_weight,
            value_weight,
            total[1],
            total[2],
            cos,
            sin,
            [embed, total[4], total[5]] if first else None,
        )
        query = finish_q(
            last,
            scalars,
            query_weight,
            total[0],
            cos,
            sin,
            code_sets[strand][0],
            total[3] if first else eq,
            embed if first else None,
        )
        return made, query

    def spread_out(own, far):
        local = [own] + far
        return local + ctx_swap(local)

    def attend_part(strand, part, cols, blocks, query, tables, before, ids):
        return attend(
            strand == 0,
            part * cols,
            cols,
            ids,
            query[0],
            query[1],
            tables,
            *code_sets[strand],
            *rope[strand],
            blocks,
            before,
        )

    arrived, partial = [[], []], []
    cut = own_chains(tie(hidden, moving), 1)
    lanes = lax.axis_size("groups") * ctx
    piece_rows = width // lanes
    lane = lax.axis_index("groups") * ctx + me
    piece = lax.dynamic_slice_in_dim(out_weight, lane * piece_rows, piece_rows, 0)
    pieces = []
    for shift in range(slabs):
        target = (head + shift) % slabs
        pieces.append(lax.dynamic_slice_in_dim(piece, target * tile, tile, 1))
    def around(item, shift):
        return lax.ppermute(item, "head", [(i, (i + shift) % slabs) for i in range(slabs)])

    pieces = [around(tie(item, moving), shift) if shift else item for shift, item in enumerate(pieces)]
    total = run_ring(0, moving, [rope, (code_sets, cut)])
    last = arrived[0][-1]
    moving = [tie(block, item) for block, item in zip(cut, last)]
    moving = hop(moving[:-1] + [tie(moving[-1], total)])
    made, query = finish(0, last, total, None, 1)
    own, tables, eq = made[0], made[1:], query[2]
    total = run_ring(1, moving, [])
    far = ctx_far(tie(own, arrived[1][0]))
    blocks = spread_out(own, tie(far, arrived[1][max(0, slabs - 3)]))
    before = attend_part(0, 0, width, blocks, query, tables, None, tie(ids, total))
    last = tie(arrived[1][-1], before)

    own_then, query_then = finish(1, last, total, eq, parts)
    far_then = [ctx_far(item) for item in own_then]
    far_then[0] = tie(far_then[0], own_then, query_then)
    pieces = tie(jnp.stack(pieces), partial[:1])
    out_slabs = lax.all_gather(pieces, ("groups", "ctx"), axis=1, tiled=True)
    combined, result = [], None
    for part in range(parts):
        blocks = spread_out(own_then[part], tie(far_then[part], combined))
        item = attend_part(1, part, cols, blocks, query_then, tables, before, ids)
        combined.append(item)
    for part, item in enumerate(combined):
        slab_rows = [around(item, shift) if shift else item for shift in range(slabs)]
        result = out_project(part, slab_rows, out_slabs, part == parts - 1, result, ids)
    return result


def solution(mesh):
    return jax.shard_map(
        shards,
        mesh=mesh,
        in_specs=(
            P(None, ("groups", "ctx"), "head"),
            P(("groups", "ctx")),
            P("groups"),
            P("groups"),
            P(),
            P(None, "head"),
            P(None, "head"),
            P(None, "head"),
            P("head", None),
        ),
        out_specs=P(("groups", "ctx"), "head"),
        check_vma=False,
    )
```

```python
import functools
import math

import jax
import jax.numpy as jnp
from jax import lax
from jax.experimental import pallas as pl
from jax.experimental.pallas import tpu as pltpu
from jax.sharding import PartitionSpec as P

HEAD_DIM = 128
BASES = 4
CODES = 16
SUM_CODE = 8
ROPE_BASE = 10000.0
NEG_FILL = -1e30
COST_CUT = 64
SCORE_SCALE = math.log2(math.e) / math.sqrt(HEAD_DIM)
VMEM_LIMIT = 24 * 1024 * 1024
WEIGHT_VMEM_LIMIT = 53 * 1024 * 1024
F32 = jnp.float32
BF16 = jnp.bfloat16


def params(limit=VMEM_LIMIT):
    return pltpu.CompilerParams(vmem_limit_bytes=limit)


def cost(flops, moved, exps=0):
    return pl.CostEstimate(
        flops=flops // COST_CUT, bytes_accessed=moved // COST_CUT, transcendentals=exps // COST_CUT
    )


def dot(left, right):
    return jnp.dot(left, right, preferred_element_type=F32)


def rope_tables(positions):
    half = HEAD_DIM // 2
    freq = jnp.power(ROPE_BASE, -jnp.arange(half, dtype=F32) * 2.0 / HEAD_DIM)
    angle = positions[:, None] * freq[None, :]
    cos, sin = jnp.cos(angle), jnp.sin(angle)
    return jnp.concatenate([cos, cos], axis=1), jnp.concatenate([-sin, sin], axis=1)


def swapped(value):
    return pltpu.roll(value, HEAD_DIM // 2, axis=1)


def turned(value, cos, sin):
    return value * cos + swapped(value) * sin


def code_table(rows):
    high = rows.astype(BF16)
    low = (rows - high.astype(F32)).astype(BF16)
    at = lax.broadcasted_iota(jnp.int32, rows.shape, 0)
    return jnp.where(at < BASES, high.astype(F32), low.astype(F32)).astype(BF16)


def read_rows(refs, strand):
    parts = [ref[strand] if len(ref.shape) == 3 else ref[...] for ref in refs]
    return parts[0] if len(parts) == 1 else jnp.concatenate(parts, axis=0)


def local_call(kernel, name, scalars, operands, far, out_shape, scratch, work):
    vmem = pl.BlockSpec(memory_space=pltpu.VMEM)
    hbm = pl.BlockSpec(memory_space=pltpu.HBM)
    return pl.pallas_call(
        kernel,
        in_specs=[pl.BlockSpec(memory_space=pltpu.SMEM)]
        + [hbm] * far
        + [vmem] * (len(operands) - far),
        out_specs=[vmem] * len(out_shape),
        out_shape=out_shape,
        scratch_shapes=scratch,
        compiler_params=params(WEIGHT_VMEM_LIMIT),
        cost_estimate=work,
        name=name,
    )(scalars, *operands)


def fetch(weight_refs, slab, held, sems):
    tile = held.shape[1]
    copies = []
    for index, weight in enumerate(weight_refs):
        first = pl.multiple_of(slab * tile, tile)
        copy = pltpu.make_async_copy(
            weight.at[pl.ds(first, tile), :], held.at[index], sems.at[index]
        )
        copy.start()
        copies.append(copy)
    return copies


def slab_kernel(strand, slab_parts, with_embed, has_total, slab_ref, *refs):
    weights, refs = refs[:3], refs[3:]
    count = len(slab_parts)
    held, sems = refs[-2:]
    refs = refs[:-2]
    copies = [fetch(weights, slab_ref[at], held.at[at], sems.at[at]) for at in range(count)]
    if with_embed:
        embed_ref, refs = refs[0], refs[1:]
    rows = []
    for parts in slab_parts:
        rows.append(read_rows(refs[:parts], strand))
        refs = refs[parts:]
    size = 6 if with_embed else 3
    totals = refs[:size] if has_total else [None] * size
    outs = refs[-size:]
    tile = held.shape[2]
    for at in range(count):
        for index in range(3):
            copies[at][index].wait()
            weight = held[at, index]
            pairs = [(index, rows[at])]
            if with_embed:
                first = pl.multiple_of(slab_ref[at] * tile, tile)
                pairs.append((3 + index, embed_ref[:, pl.ds(first, tile)]))
            for slot, left in pairs:
                item = dot(left, weight)
                if at:
                    item = outs[slot][...] + item
                elif has_total:
                    item = totals[slot][...] + item
                outs[slot][...] = item


def slab_sums(slabs, scalars, strand, weights, embed=None, total=None):
    width = weights[0].shape[1]
    tile = slabs[0][0].shape[-1]
    rows = sum(x.shape[-2] for x in slabs[0])
    operands = [*weights] + ([embed] if embed is not None else [])
    for parts in slabs:
        operands += parts
    if total is not None:
        operands += total
    heights = [rows] * 3 + ([CODES] * 3 if embed is not None else [])
    return local_call(
        functools.partial(
            slab_kernel,
            strand,
            [len(parts) for parts in slabs],
            embed is not None,
            total is not None,
        ),
        "slab_sums",
        scalars,
        operands,
        3,
        [jax.ShapeDtypeStruct((height, width), F32) for height in heights],
        [
            pltpu.VMEM((len(slabs), 3, tile, width), BF16),
            pltpu.SemaphoreType.DMA((len(slabs), 3)),
        ],
        cost(6 * rows * tile * width * len(slabs), 6 * tile * width * len(slabs)),
    )


def finish_kv_kernel(x_count, part_count, with_embed, scalars, *refs):
    weights, refs = refs[:2], refs[2:]
    held, sems = refs[-2:]
    copies = fetch(weights, scalars[0], held, sems)
    x_refs, refs = refs[:x_count], refs[x_count:]
    (ksum_ref, vsum_ref, cos_ref, sin_ref), refs = refs[:4], refs[4:]
    if with_embed:
        (embed_ref, ek_ref, ev_ref), refs = refs[:3], refs[3:]
    kv_refs, refs = refs[:part_count], refs[part_count:]
    tile = held.shape[1]
    rows = read_rows(x_refs, 0)
    height, width = ksum_ref.shape
    part_cols = width // part_count
    own = pl.ds(pl.multiple_of(scalars[1] * height, height), height)
    cos, sin = cos_ref[own, :], sin_ref[own, :]
    if with_embed:
        embed = embed_ref[:, pl.ds(pl.multiple_of(scalars[0] * tile, tile), tile)]
        table_ref, swapped_ref, ev_out = refs[:3]
    copies[0].wait()
    key = ksum_ref[...] + dot(rows, held[0])
    for start in range(0, width, HEAD_DIM):
        part, at = start // part_cols, start % part_cols
        turned_key = turned(key[:, start : start + HEAD_DIM], cos, sin)
        kv_refs[part][0, :, at : at + HEAD_DIM] = turned_key.astype(BF16)
    if with_embed:
        ek = ek_ref[...] + dot(embed, held[0])
        table_ref[...] = code_table(ek)
        for start in range(0, width, HEAD_DIM):
            cols = slice(start, start + HEAD_DIM)
            swapped_ref[:, cols] = code_table(swapped(ek[:, cols]))
    copies[1].wait()
    value = vsum_ref[...] + dot(rows, held[1])
    for part in range(part_count):
        kv_refs[part][1] = value[:, part * part_cols : (part + 1) * part_cols].astype(BF16)
    if with_embed:
        ev_out[...] = ev_ref[...] + dot(embed, held[1])


def finish_kv(part_count, x_parts, scalars, wk, wv, ksum, vsum, cos, sin, embed_parts):
    tile = x_parts[0].shape[-1]
    rows, width = ksum.shape
    operands = [wk, wv, *x_parts, ksum, vsum, cos, sin]
    out_shape = [jax.ShapeDtypeStruct((2, rows, width // part_count), BF16)] * part_count
    if embed_parts is not None:
        operands += embed_parts
        out_shape += [jax.ShapeDtypeStruct((CODES, width), kind) for kind in (BF16, BF16, F32)]
    return local_call(
        functools.partial(finish_kv_kernel, len(x_parts), part_count, embed_parts is not None),
        "finish_kv",
        scalars,
        operands,
        2,
        out_shape,
        [pltpu.VMEM((2, tile, width), BF16), pltpu.SemaphoreType.DMA((2,))],
        cost(4 * rows * tile * width, 4 * tile * width + 14 * rows * width),
    )


def finish_q_kernel(x_count, with_embed, scalars, *refs):
    weights, refs = refs[:1], refs[1:]
    held, sems = refs[-2:]
    copies = fetch(weights, scalars[0], held, sems)
    x_refs, refs = refs[:x_count], refs[x_count:]
    (qsum_ref, cos_ref, sin_ref, codes_ref, eq_ref), refs = refs[:5], refs[5:]
    tile = held.shape[1]
    height, width = qsum_ref.shape
    own = pl.ds(pl.multiple_of(scalars[1] * height, height), height)
    cos, sin = cos_ref[own, :] * SCORE_SCALE, sin_ref[own, :] * SCORE_SCALE
    rows = read_rows(x_refs, 0)
    copies[0].wait()
    eq = eq_ref[...]
    if with_embed:
        embed_ref, q_ref, qm_ref, eq_out = refs[:4]
        first = pl.multiple_of(scalars[0] * tile, tile)
        eq = eq + dot(embed_ref[:, pl.ds(first, tile)], held[0])
        eq_out[...] = eq
    else:
        q_ref, qm_ref = refs[:2]
    query = qsum_ref[...] + dot(rows, held[0])
    mutant = query + dot(codes_ref[0], code_table(eq))
    for start in range(0, width, HEAD_DIM):
        cols = slice(start, start + HEAD_DIM)
        q_ref[:, cols] = turned(query[:, cols], cos, sin).astype(BF16)
        qm_ref[:, cols] = turned(mutant[:, cols], cos, sin).astype(BF16)


def finish_q(x_parts, scalars, wq, qsum, cos, sin, codes, eq, embed):
    tile = x_parts[0].shape[-1]
    rows, width = qsum.shape
    operands = [wq, *x_parts, qsum, cos, sin, codes, eq]
    out_shape = [jax.ShapeDtypeStruct((rows, width), BF16)] * 2
    if embed is not None:
        operands.append(embed)
        out_shape.append(jax.ShapeDtypeStruct((CODES, width), F32))
    return local_call(
        functools.partial(finish_q_kernel, len(x_parts), embed is not None),
        "finish_q",
        scalars,
        operands,
        1,
        out_shape,
        [pltpu.VMEM((1, tile, width), BF16), pltpu.SemaphoreType.DMA((1,))],
        cost(2 * rows * tile * width, 2 * tile * width + 8 * rows * width),
    )


def attend_kernel(forward, block_count, has_before, q_start, table_start, before_start, *refs):
    (ids_ref, q_ref, qm_ref, table_ref, swapped_ref, ev_ref), refs = refs[:6], refs[6:]
    (codes_ref, codes_t_ref, cos_ref, sin_ref), refs = refs[:4], refs[4:]
    kv_refs, refs = refs[:block_count], refs[block_count:]
    before_ref = None
    if has_before:
        before_ref, refs = refs[0], refs[1:]
    out_ref, top, acc = refs
    rows, cols_here = out_ref.shape
    heads = cols_here // HEAD_DIM
    tall = HEAD_DIM + CODES
    my_id = ids_ref[0]

    def block(index):
        kv_ref = kv_refs[index]
        first = pl.multiple_of(ids_ref[index] * rows, rows)
        cos = cos_ref[pl.ds(first, rows), :]
        sin = sin_ref[pl.ds(first, rows), :]
        codes, codes_t = codes_ref[index], codes_t_ref[index]
        here = slice(table_start, table_start + cols_here)
        change = dot(codes, table_ref[:, here])
        change_swapped = dot(codes, swapped_ref[:, here])
        if index == 0:
            key_at = lax.broadcasted_iota(jnp.int32, (rows, rows), 0)
            query_at = lax.broadcasted_iota(jnp.int32, (rows, rows), 1)
            seen = key_at <= query_at if forward else key_at >= query_at
        scores, values = [], []
        for head in range(heads):
            cols = slice(head * HEAD_DIM, (head + 1) * HEAD_DIM)
            q_cols = slice(q_start + cols.start, q_start + cols.stop)
            key = kv_ref[0, :, cols]
            mutant_key = (
                key.astype(F32) + change[:, cols] * cos + change_swapped[:, cols] * sin
            ).astype(BF16)
            values.append(jnp.concatenate([kv_ref[1, :, cols].T, codes_t], axis=0))
            for query, keys in ((q_ref[:, q_cols], key), (qm_ref[:, q_cols], mutant_key)):
                scores.append(
                    lax.dot_general(
                        keys, query, (((1,), (1,)), ((), ())), preferred_element_type=F32
                    )
                )
        fades, weights = [], []
        for unit, score in enumerate(scores):
            if index == 0:
                score = jnp.where(seen, score, NEG_FILL)
            peak = jnp.max(score, axis=0, keepdims=True)
            if index:
                old_peak = top[unit : unit + 1, :]
                peak = jnp.maximum(old_peak, peak)
                fades.append(jnp.exp2(old_peak - peak))
            top[unit : unit + 1, :] = peak
            weights.append(jnp.exp2(score - peak).astype(BF16))
        for unit, weight in enumerate(weights):
            area = slice(unit * tall, (unit + 1) * tall)
            product = dot(values[unit // 2], weight)
            acc[area, :] = acc[area, :] * fades[unit] + product if index else product

    for index in range(block_count):
        if index == 0:
            block(0)
        else:
            other = ids_ref[index]
            pl.when(other < my_id if forward else other > my_id)(functools.partial(block, index))

    code_at = lax.broadcasted_iota(jnp.int32, (CODES, HEAD_DIM), 0)
    for head in range(heads):
        cols = slice(head * HEAD_DIM, (head + 1) * HEAD_DIM)
        table_cols = slice(table_start + cols.start, table_start + cols.stop)
        ev = jnp.where(code_at < BASES, ev_ref[:, table_cols], 0.0)
        parts = []
        for kind in range(2):
            start = (2 * head + kind) * tall
            value = acc[start : start + HEAD_DIM, :]
            tail = acc[start + HEAD_DIM : start + tall, :]
            if kind:
                value = value + lax.dot_general(
                    ev,
                    tail,
                    (((0,), (0,)), ((), ())),
                    precision=lax.Precision.HIGHEST,
                    preferred_element_type=F32,
                )
            parts.append(value / tail[SUM_CODE : SUM_CODE + 1, :])
        difference = (parts[0] - parts[1]).T
        if has_before:
            earlier = before_ref[:, before_start + cols.start : before_start + cols.stop]
            out_ref[:, cols] = (0.5 * (earlier + difference)).astype(BF16)
        else:
            out_ref[:, cols] = difference


def attend(forward, start, cols, ids, q, qm, tables, codes, codes_t, cos, sin, kv_blocks, before):
    rows = q.shape[0]
    heads = cols // HEAD_DIM
    vmem = pl.BlockSpec(memory_space=pltpu.VMEM)
    operands = [q, qm, *tables, codes, codes_t, cos, sin, *kv_blocks]
    if before is not None:
        operands.append(before)
    count = len(kv_blocks)
    return pl.pallas_call(
        functools.partial(
            attend_kernel, forward, count, before is not None, start, start, start
        ),
        in_specs=[pl.BlockSpec(memory_space=pltpu.SMEM)] + [vmem] * len(operands),
        out_specs=vmem,
        out_shape=jax.ShapeDtypeStruct((rows, cols), F32 if before is None else BF16),
        scratch_shapes=[
            pltpu.VMEM((max(2 * heads, 8), rows), F32),
            pltpu.VMEM((2 * heads * (HEAD_DIM + CODES), rows), F32),
        ],
        compiler_params=params(),
        cost_estimate=cost(
            8 * rows * rows * count * cols,
            4 * count * rows * cols,
            2 * rows * rows * count * heads,
        ),
        name="attend_forward" if forward else "attend_reverse",
    )(ids, *operands)


def out_kernel(part, slabs, has_before, scalars, weight_ref, *refs):
    del scalars
    held, sems = refs[-2:]
    out_ref = refs[-3]
    row_refs = refs[:slabs]
    cols = held.shape[1]
    copies = []
    for index in range(slabs):
        copy = pltpu.make_async_copy(
            weight_ref.at[index, pl.ds(part * cols, cols), :], held.at[index], sems.at[index]
        )
        copy.start()
        copies.append(copy)
    total = refs[slabs][...] if has_before else None
    for index in range(slabs):
        copies[index].wait()
        item = dot(row_refs[index][...], held[index])
        total = item if total is None else total + item
    out_ref[...] = total.astype(out_ref.dtype)


def out_project(part, slab_rows, weight, last, before, scalars):
    slabs = len(slab_rows)
    rows, cols = slab_rows[0].shape
    width = weight.shape[2]
    operands = [weight, *slab_rows] + ([before] if before is not None else [])
    return local_call(
        functools.partial(out_kernel, part, slabs, before is not None),
        "out_project",
        scalars,
        operands,
        1,
        [jax.ShapeDtypeStruct((rows, width), BF16 if last else F32)],
        [pltpu.VMEM((slabs, cols, width), BF16), pltpu.SemaphoreType.DMA((slabs,))],
        cost(2 * slabs * rows * cols * width, 2 * slabs * cols * width),
    )[0]


def shards(
    hidden,
    strand_bases,
    variant_sites,
    base_shift,
    base_embed,
    query_weight,
    key_weight,
    value_weight,
    out_weight,
):
    rows, tile = hidden.shape[1:]
    ctx = lax.axis_size("ctx")
    slabs = lax.axis_size("head")
    me = lax.axis_index("ctx")
    head = lax.axis_index("head")
    window = rows * ctx
    width = query_weight.shape[1]
    cores = 2 if ctx % 2 == 0 else 1
    chains = 2 if rows % 32 == 0 else 1
    parts = 2 if width % (2 * HEAD_DIM) == 0 else 1
    cols = width // parts
    weights = (query_weight, key_weight, value_weight)
    my_row = me.astype(jnp.int32)
    ring = [(i, (i + 1) % slabs) for i in range(slabs)]
    slab_at = [((head - step) % slabs).astype(jnp.int32) for step in range(slabs)]

    def tie(items, *first):
        return lax.optimization_barrier((items, first))[0]

    def ctx_far(block):
        return [
            lax.ppermute(block, "ctx", [(i, (i + cores * shift) % ctx) for i in range(ctx)])
            for shift in range(1, ctx // cores)
        ]

    def ctx_swap(blocks):
        if cores == 1:
            return []
        return [lax.ppermute(item, "ctx", [(i, i ^ 1) for i in range(ctx)]) for item in blocks]

    def hop(blocks):
        return [lax.ppermute(block, "head", ring) for block in blocks]

    near = [(me - cores * shift) % ctx for shift in range(ctx // cores)]
    if cores == 2:
        near = near + [item ^ 1 for item in near]
    ids = jnp.stack(near).astype(jnp.int32)

    span = rows // chains

    def own_chains(source, strand):
        return [source[strand, chain * span : (chain + 1) * span] for chain in range(chains)]

    moving = hop(own_chains(hidden, 0))

    bases = [strand_bases] + ctx_far(strand_bases)
    bases = jnp.stack(bases + ctx_swap(bases))
    positions = ids[:, None] * rows + jnp.arange(rows, dtype=jnp.int32)[None, :]
    match = positions[:, :, None] == variant_sites[None, None, :]
    shifts = jnp.sum(jnp.where(match, base_shift[None, None, :], 0), axis=2)
    fresh = jnp.mod(bases + shifts, BASES)
    code_iota = jnp.arange(CODES, dtype=jnp.int32)

    def code_arrays(forward):
        want = code_iota % BASES
        want = want if forward else BASES - 1 - want

        def fill(old, new, want, at):
            codes = (new == want).astype(F32) - (old == want).astype(F32)
            codes = jnp.where(at < 2 * BASES, codes, (at == SUM_CODE).astype(F32))
            return codes.astype(BF16)

        return (
            fill(bases[:, :, None], fresh[:, :, None], want, code_iota),
            fill(bases[:, None, :], fresh[:, None, :], want[:, None], code_iota[:, None]),
        )

    embed = jnp.concatenate(
        [base_embed, base_embed, jnp.zeros((CODES - 2 * BASES, base_embed.shape[1]), BF16)]
    )
    window_iota = jnp.arange(window, dtype=jnp.int32)
    rope = [
        rope_tables(window_iota.astype(F32)),
        rope_tables((window - 1 - window_iota).astype(F32)),
    ]

    code_sets = [code_arrays(True), code_arrays(False)]

    def add_slabs(strand, steps, total):
        return slab_sums(
            [[hidden] if step == 0 else arrived[strand][step - 1] for step in steps],
            jnp.stack([slab_at[step] for step in steps]),
            strand,
            weights,
            embed if strand == 0 else None,
            total,
        )

    def run_ring(strand, moving, early):
        total, waiting = None, [0]
        partial.clear()
        for step in range(1, slabs):
            arrived[strand].append(moving)
            if step < slabs - 1:
                first = (early.pop(0) if early else None, total)
                moving = hop(moving[:-1] + [tie(moving[-1], first)])
                waiting.append(step)
                total = add_slabs(strand, waiting, total)
                partial.append(total)
                waiting = []
        if waiting:
            total = add_slabs(strand, waiting, total)
        return total

    def finish(strand, last, total, eq, count):
        first = strand == 0
        cos, sin = rope[strand]
        scalars = jnp.stack([slab_at[-1], my_row])
        made = finish_kv(
            count,
            last,
            scalars,
            key_weight,
            value_weight,
            total[1],
            total[2],
            cos,
            sin,
            [embed, total[4], total[5]] if first else None,
        )
        query = finish_q(
            last,
            scalars,
            query_weight,
            total[0],
            cos,
            sin,
            code_sets[strand][0],
            total[3] if first else eq,
            embed if first else None,
        )
        return made, query

    def spread_out(own, far):
        local = [own] + far
        return local + ctx_swap(local)

    def attend_part(strand, part, cols, blocks, query, tables, before, ids):
        return attend(
            strand == 0,
            part * cols,
            cols,
            ids,
            query[0],
            query[1],
            tables,
            *code_sets[strand],
            *rope[strand],
            blocks,
            before,
        )

    arrived, partial = [[], []], []
    cut = own_chains(tie(hidden, moving), 1)
    lanes = lax.axis_size("groups") * ctx
    piece_rows = width // lanes
    lane = lax.axis_index("groups") * ctx + me
    piece = lax.dynamic_slice_in_dim(out_weight, lane * piece_rows, piece_rows, 0)
    pieces = []
    for shift in range(slabs):
        target = (head + shift) % slabs
        pieces.append(lax.dynamic_slice_in_dim(piece, target * tile, tile, 1))
    def around(item, shift):
        return lax.ppermute(item, "head", [(i, (i + shift) % slabs) for i in range(slabs)])

    pieces = [around(tie(item, moving), shift) if shift else item for shift, item in enumerate(pieces)]
    total = run_ring(0, moving, [rope, (code_sets, cut, pieces)])
    last = arrived[0][-1]
    moving = [tie(block, item) for block, item in zip(cut, last)]
    moving = hop(moving[:-1] + [tie(moving[-1], total)])
    made, query = finish(0, last, total, None, 1)
    own, tables, eq = made[0], made[1:], query[2]
    far = ctx_far(own)

    total = run_ring(1, moving, [(own,)])
    blocks = spread_out(own, tie(far, arrived[1][0]))
    before = attend_part(0, 0, width, blocks, query, tables, None, tie(ids, total))
    last = tie(arrived[1][-1], before)

    own_then, query_then = finish(1, last, total, eq, parts)
    far_then = [ctx_far(item) for item in own_then]
    far_then[0] = tie(far_then[0], own_then, query_then)
    pieces = tie(jnp.stack(pieces), own)
    out_slabs = lax.all_gather(pieces, ("groups", "ctx"), axis=1, tiled=True)
    combined, result = [], None
    for part in range(parts):
        blocks = spread_out(own_then[part], tie(far_then[part], combined))
        item = attend_part(1, part, cols, blocks, query_then, tables, before, ids)
        combined.append(item)
    for part, item in enumerate(combined):
        slab_rows = [around(item, shift) if shift else item for shift in range(slabs)]
        result = out_project(part, slab_rows, out_slabs, part == parts - 1, result, ids)
    return result


def solution(mesh):
    return jax.shard_map(
        shards,
        mesh=mesh,
        in_specs=(
            P(None, ("groups", "ctx"), "head"),
            P(("groups", "ctx")),
            P("groups"),
            P("groups"),
            P(),
            P(None, "head"),
            P(None, "head"),
            P(None, "head"),
            P("head", None),
        ),
        out_specs=P(("groups", "ctx"), "head"),
        check_vma=False,
    )
```
